32 devices in a mesh: fsdp: 2 (over x), ctx: 4 (over z), tp: 4 (over y, core).
Axes of the slice: x: 2, y: 2, z: 4, core: 2. Of those that a mesh axis runs over, the one named last changes fastest.
Arguments:
- hidden_in: bfloat16 [5120, 2048], P(('fsdp', 'ctx')), may hold values from -6 to 6
- teacher: bfloat16 [5120, 2048], P(('fsdp', 'ctx')), may hold values from -6 to 6
- w_query: bfloat16 [2048, 2048], P('fsdp', 'tp'), may hold values from -0.125 to 0.125
- w_key: bfloat16 [2048, 1024], P('fsdp', 'tp'), may hold values from -0.125 to 0.125
- w_value: bfloat16 [2048, 1024], P('fsdp', 'tp'), may hold values from -0.125 to 0.125
- w_out: bfloat16 [2048, 2048], P('tp', 'fsdp'), may hold values from -0.75 to 0.75
- w_gate: bfloat16 [2048, 8192], P('fsdp', 'tp'), may hold values from -0.125 to 0.125
- w_up: bfloat16 [2048, 8192], P('fsdp', 'tp'), may hold values from -0.125 to 0.125
- w_down: bfloat16 [8192, 2048], P('tp', 'fsdp'), may hold values from -0.0625 to 0.0625
- attn_gain: bfloat16 [2048], P('fsdp'), may hold values from 0.5 to 1.5
- ffn_gain: bfloat16 [2048], P('fsdp'), may hold values from 0.5 to 1.5
- segment_ids: int32 [5120], P(('fsdp', 'ctx')), may hold values from 0 to 25, as said below
- parents: int32 [26], replicated, may hold values from -1 to 25, as said below
- positions: int32 [5120], P(('fsdp', 'ctx')), may hold values from 0 to 1279, as said below
- valid_mask: int32 [5120], P(('fsdp', 'ctx')), may hold values from 0 to 1, as said below
Outputs:
- output: bfloat16 [5120, 2048], P(('fsdp', 'ctx'))
- mean_loss: float32 [], replicated
- grad_hidden: float32 [5120, 2048], P(('fsdp', 'ctx'))
- grad_w_query: float32 [2048, 2048], P('fsdp', 'tp')
- grad_w_key: float32 [2048, 1024], P('fsdp', 'tp')
- grad_w_value: float32 [2048, 1024], P('fsdp', 'tp')
- grad_w_out: float32 [2048, 2048], P('tp', 'fsdp')
- grad_w_gate: float32 [2048, 8192], P('fsdp', 'tp')
- grad_w_up: float32 [2048, 8192], P('fsdp', 'tp')
- grad_w_down: float32 [8192, 2048], P('tp', 'fsdp')
- grad_attn_gain: float32 [2048], P('fsdp')
- grad_ffn_gain: float32 [2048], P('fsdp')
The draws below stay inside these ranges and needn't reach their ends.
Inputs may be any that keep to these rules, and one draw needn't show every extreme that they name: `segment_ids`: tree t fills slots t * 2560 onward and has segments t * 13 to t * 13 + 12 in some numbering: its trunk holds the first 1024 slots, then twelve runs of 128 slots each hold one whole segment, four branches and eight leaves, in any order. `parents`: entry s is the parent of segment s: -1 for a trunk, the trunk of its tree for a branch, a branch of its tree for a leaf, two leaves to each branch. `positions`: trunk slots count 0 up in order; the j-th token of a branch has 1024 + j, of a leaf 9 * 128 + j. `valid_mask`: 0 on exactly the slots of one or two whole absent leaves in each tree, 1 elsewhere.
All inputs are finite; a program needn't handle non-finite values.
Results may differ from the reference program's by a relative error of at most 0.01.
The reference program's roundings to bfloat16 on the way count: a program that leaves them out, or rounds other values in their place, can miss the bound.
Values may be sent and summed in bfloat16 or wider, within the bound.
No kernel may reach another device: no remote copies, remote signals or barrier semaphores. Data moves between devices by JAX's collectives and lax.ppermute only.
A program may use at most 256 MiB of HBM per device.

```python
import math
import jax
import jax.numpy as jnp
from jax import lax

D = 2048
H = 16
KV = 8
HD = 128
FF = 8192
NSEG = 13
TREES = 2
UNIT = 128
TOKENS = 5120
KBLOCK = 512


def tree_layout(key, tree_index):
    seeded = jax.random.fold_in(key, 7001 + tree_index)
    subkeys = jax.random.split(seeded, 4)
    labels = jax.random.permutation(subkeys[0], NSEG).astype(jnp.int32)
    run_order = jax.random.permutation(subkeys[1], NSEG - 1).astype(jnp.int32)
    missing = jax.random.randint(subkeys[2], (), 1, 3).astype(jnp.int32)
    leaf_rank = jax.random.permutation(subkeys[3], 8).astype(jnp.int32)
    slot_ids = jnp.arange(20 * UNIT, dtype=jnp.int32)
    run_index = slot_ids // UNIT
    run_offset = slot_ids % UNIT
    in_trunk = run_index < 8
    member = run_order[jnp.clip(run_index - 8, 0, NSEG - 2)]
    local_seg = jnp.where(in_trunk, labels[0], labels[member + 1])
    depth = jnp.where(in_trunk, slot_ids, jnp.where(member < 4, 8 * UNIT + run_offset, 9 * UNIT + run_offset))
    leaf_absent = leaf_rank < missing
    slot_absent = jnp.logical_and(jnp.logical_not(in_trunk), jnp.logical_and(member >= 4, leaf_absent[jnp.clip(member - 4, 0, 7)]))
    present = jnp.where(slot_absent, 0, 1).astype(jnp.int32)
    tree_offset = tree_index * NSEG
    parent_rows = jnp.concatenate([jnp.full((1,), -1, jnp.int32), jnp.zeros((4,), jnp.int32) + labels[0], labels[1 + jnp.arange(8, dtype=jnp.int32) // 2]])
    parent_rows = jnp.where(parent_rows < 0, -1, parent_rows + tree_offset).astype(jnp.int32)
    parent_table = jnp.zeros((NSEG,), jnp.int32).at[labels].set(parent_rows)
    return ((local_seg + tree_offset).astype(jnp.int32), depth.astype(jnp.int32), present, parent_table)


def draw_segment_ids(key, part):
    return jnp.concatenate([tree_layout(key, tree_index)[0] for tree_index in range(TREES)])


def draw_positions(key, part):
    return jnp.concatenate([tree_layout(key, tree_index)[1] for tree_index in range(TREES)])


def draw_valid_mask(key, part):
    return jnp.concatenate([tree_layout(key, tree_index)[2] for tree_index in range(TREES)])


def draw_parents(key, part):
    return jnp.concatenate([tree_layout(key, tree_index)[3] for tree_index in range(TREES)])


def levels(own_key, extent, shards, low, top_value):
    def one(position, parts):
        draws = jax.random.uniform(jax.random.fold_in(jax.random.fold_in(own_key, 6), position), (parts,), jnp.float32, low / len(shards), top_value / len(shards))
        return jnp.repeat(jnp.exp(draws), extent[position] // parts).reshape((-1,) + (1,) * (len(extent) - position - 1))

    factor_of = one(*shards[0])
    for cut in shards[1:]:
        factor_of = factor_of * one(*cut)
    return factor_of


def centred(rng, dims, scale, limit, cuts=(), kind=jnp.bfloat16):
    level = levels(rng, dims, cuts, -0.22, 0.18) if cuts else 1.0
    values = jax.random.normal(rng, dims, jnp.float32) * scale * level
    return jnp.minimum(jnp.maximum(values, -limit), limit).astype(kind)


def setup_inputs(seed: int = 0) -> dict:
    seeds = jax.random.split(jax.random.key(seed), 16)
    return {
        "hidden_in": centred(seeds[0], (TOKENS, D), 1.0, 6.0, ((0, 8),)),
        "teacher": centred(seeds[1], (TOKENS, D), 1.0, 6.0, ((0, 8),)),
        "w_query": centred(seeds[2], (D, H * HD), D ** -0.5, 0.125, ((0, 2), (1, 4))),
        "w_key": centred(seeds[3], (D, KV * HD), D ** -0.5, 0.125, ((0, 2), (1, 4))),
        "w_value": centred(seeds[4], (D, KV * HD), D ** -0.5, 0.125, ((0, 2), (1, 4))),
        "w_out": centred(seeds[5], (H * HD, D), (H * HD // 32) ** -0.5, 0.75, ((0, 4), (1, 2))),
        "w_gate": centred(seeds[6], (D, FF), D ** -0.5, 0.125, ((0, 2), (1, 4))),
        "w_up": centred(seeds[7], (D, FF), D ** -0.5, 0.125, ((0, 2), (1, 4))),
        "w_down": centred(seeds[8], (FF, D), FF ** -0.5, 0.0625, ((0, 4), (1, 2))),
        "attn_gain": jnp.clip(1.0 + 0.1 * jax.random.normal(seeds[9], (D,), jnp.float32), 0.5, 1.5).astype(jnp.bfloat16),
        "ffn_gain": jnp.clip(1.0 + 0.1 * jax.random.normal(seeds[10], (D,), jnp.float32), 0.5, 1.5).astype(jnp.bfloat16),
        "segment_ids": draw_segment_ids(jax.random.fold_in(seeds[15], 71), 0),
        "parents": draw_parents(jax.random.fold_in(seeds[15], 71), 0),
        "positions": draw_positions(jax.random.fold_in(seeds[15], 71), 0),
        "valid_mask": draw_valid_mask(jax.random.fold_in(seeds[15], 71), 0),
    }


@jax.custom_vjp
def low(v):
    return lax.optimization_barrier(v.astype(jnp.bfloat16)).astype(jnp.float32)

@jax.custom_vjp
def low_back(v):
    return v

def low_keep(v):
    return (low(v), None)

def low_pass(kept, grad):
    return (grad,)

def back_keep(v):
    return (v, None)

def back_low(kept, grad):
    return (low(grad),)
low.defvjp(low_keep, low_pass)
low_back.defvjp(back_keep, back_low)
epsilon = 1e-05
rope_base = 1000000.0
highest = lax.Precision.HIGHEST

def rms_scale(values, gain):
    return values * lax.rsqrt(lax.optimization_barrier(jnp.mean(values * values, axis=-1, keepdims=True)) + epsilon) * gain

def rope_angles(positions, width):
    steps = jnp.arange(width // 2, dtype=jnp.float32)
    inverse = jnp.power(rope_base, -2.0 * steps / width)
    return positions.astype(jnp.float32)[:, None] * inverse[None, :]

def rotary(values, angles):
    half_width = values.shape[-1] // 2
    cosine = jnp.cos(angles)[:, None, :]
    sine_part = jnp.sin(angles)[:, None, :]
    first_half = values[..., :half_width]
    second_half = values[..., half_width:]
    return jnp.concatenate([first_half * cosine - second_half * sine_part, second_half * cosine + first_half * sine_part], axis=-1)

def ancestry(segment_ids, parents):
    labels = jnp.arange(parents.shape[0], dtype=jnp.int32)
    parent_of = lax.optimization_barrier(jnp.sum(jnp.where(segment_ids[:, None] == labels[None, :], parents[None, :], 0), axis=1)).astype(jnp.int32)
    grand_raw = lax.optimization_barrier(jnp.sum(jnp.where(parent_of[:, None] == labels[None, :], parents[None, :], 0), axis=1)).astype(jnp.int32)
    grand_of = jnp.where(parent_of < 0, -1, grand_raw).astype(jnp.int32)
    return (parent_of, grand_of)

def allowed_pairs(query_seg, query_parent, query_grand, query_place, key_seg, key_valid, key_place):
    same_seg = (key_seg[None, :] == query_seg[:, None]) & (key_place[None, :] <= query_place[:, None])
    ancestor_hit = (key_seg[None, :] == query_parent[:, None]) | (key_seg[None, :] == query_grand[:, None])
    return (key_valid[None, :] == 1) & (same_seg | ancestor_hit)

def pick_tree(array, index):
    return lax.dynamic_index_in_dim(array, index, 0, keepdims=False)

def reference(hidden_in, teacher, w_query, w_key, w_value, w_out, w_gate, w_up, w_down, attn_gain, ffn_gain, segment_ids, parents, positions, valid_mask):
    tokens = hidden_in.shape[0]
    width = hidden_in.shape[1]
    loss_factor = float(width * tokens // 2)
    tree_len = tokens // TREES
    block_count = tree_len // KBLOCK
    per_group = H // KV
    score_scale = 1.0 / math.sqrt(HD)
    angles = rope_angles(positions, HD)
    parent_of, grand_of = ancestry(segment_ids, parents)
    seg_trees = segment_ids.reshape(TREES, tree_len)
    parent_trees = parent_of.reshape(TREES, tree_len)
    grand_trees = grand_of.reshape(TREES, tree_len)
    valid_trees = valid_mask.reshape(TREES, tree_len)
    valid_f = valid_mask.astype(jnp.float32)
    teacher_f = teacher.astype(jnp.float32)
    key_place = jnp.arange(tree_len, dtype=jnp.int32)

    def attend(query, keys_all, values_all):
        query_trees = query.reshape(TREES, tree_len, KV, per_group, HD)
        key_trees = keys_all.reshape(TREES, tree_len, KV, HD)
        value_trees = values_all.reshape(TREES, tree_len, KV, HD)

        def one_block(index):
            tree_index = index // block_count
            row_start = index % block_count * KBLOCK
            query_blk = lax.dynamic_slice_in_dim(pick_tree(query_trees, tree_index), row_start, KBLOCK, 0)
            query_seg = lax.dynamic_slice_in_dim(pick_tree(seg_trees, tree_index), row_start, KBLOCK, 0)
            query_parent = lax.dynamic_slice_in_dim(pick_tree(parent_trees, tree_index), row_start, KBLOCK, 0)
            query_grand = lax.dynamic_slice_in_dim(pick_tree(grand_trees, tree_index), row_start, KBLOCK, 0)
            query_place = row_start + jnp.arange(KBLOCK, dtype=jnp.int32)
            allowed = allowed_pairs(query_seg, query_parent, query_grand, query_place, pick_tree(seg_trees, tree_index), pick_tree(valid_trees, tree_index), key_place)
            scores = low_back(jnp.einsum('rkgd,skd->kgrs', query_blk, pick_tree(key_trees, tree_index), precision=highest) * score_scale)
            unnormed = jnp.where(allowed[None, None], jnp.exp(scores), 0.0)
            row_total = lax.optimization_barrier(jnp.sum(unnormed, axis=-1))
            accumulated = low_back(jnp.einsum('kgrs,skd->kgrd', low(unnormed), pick_tree(value_trees, tree_index), precision=highest))
            context = accumulated / row_total[..., None]
            return context.transpose(2, 0, 1, 3).reshape(KBLOCK, H * HD)
        results = lax.map(jax.checkpoint(one_block), jnp.arange(TREES * block_count, dtype=jnp.int32))
        return results.reshape(tokens, H * HD)

    def forward(hidden, query_w, key_w, value_w, out_w, gate_w, up_w, down_w, gain_attn, gain_ffn):
        normed = low(rms_scale(hidden, gain_attn))
        query_pre = low_back(jnp.dot(normed, query_w, precision=highest)).reshape(tokens, H, HD)
        key_pre = low_back(jnp.dot(normed, key_w, precision=highest)).reshape(tokens, KV, HD)
        query = low(rotary(query_pre, angles))
        keys_all = low(rotary(key_pre, angles))
        values_all = low(low_back(jnp.dot(normed, value_w, precision=highest))).reshape(tokens, KV, HD)
        attended = low(attend(query, keys_all, values_all))
        attn_out = low_back(jnp.dot(attended, out_w, precision=highest))
        middle = hidden + attn_out
        normed_ffn = low(rms_scale(middle, gain_ffn))
        gate_proj = low_back(jnp.dot(normed_ffn, gate_w, precision=highest))
        up_proj = low_back(jnp.dot(normed_ffn, up_w, precision=highest))
        activated = low(jax.nn.silu(gate_proj) * up_proj)
        output_f = middle + low_back(jnp.dot(activated, down_w, precision=highest))
        deviation = output_f - teacher_f
        loss_value = jnp.sum(valid_f * lax.optimization_barrier(jnp.mean(deviation * deviation, axis=1))) / jnp.sum(valid_f)
        return (loss_value * loss_factor, (output_f, loss_value))
    primals = (hidden_in.astype(jnp.float32), w_query.astype(jnp.float32), w_key.astype(jnp.float32), w_value.astype(jnp.float32), w_out.astype(jnp.float32), w_gate.astype(jnp.float32), w_up.astype(jnp.float32), w_down.astype(jnp.float32), attn_gain.astype(jnp.float32), ffn_gain.astype(jnp.float32))
    scaled, vjp_fn, aux_pair = jax.vjp(forward, *primals, has_aux=True)
    grads = vjp_fn(jnp.ones_like(scaled))
    output_f, loss_value = aux_pair
    return (output_f.astype(jnp.bfloat16), loss_value, grads[0], grads[1], grads[2], grads[3], grads[4], grads[5], grads[6], grads[7], grads[8], grads[9])
```

```python
from functools import partial
import math

import jax
import jax.numpy as jnp
from jax import lax
from jax.experimental import pallas as pl
from jax.experimental.pallas import tpu as pltpu
from jax.sharding import PartitionSpec as P

HD = 128
BLK = 128
EPSILON = 1e-05
ROPE_BASE = 1000000.0
SCALE = 1.0 / math.sqrt(HD)
F32 = jnp.float32
BF16 = jnp.bfloat16
VMEM_LIMIT = 56 * 1024 * 1024
BIG = 1 << 30


def swap_x(a):
    return lax.ppermute(a, "fsdp", [(0, 1), (1, 0)])


def swap_core(a):
    return lax.ppermute(a, "tp", [(0, 1), (1, 0), (2, 3), (3, 2)])


def swap_y(a):
    return lax.ppermute(a, "tp", [(0, 2), (2, 0), (1, 3), (3, 1)])


def swap_xy(a):
    pairs = [(f * 4 + t, (1 - f) * 4 + (t ^ 2)) for f in range(2) for t in range(4)]
    return lax.ppermute(a, ("fsdp", "tp"), pairs)


def after(value, *others):
    return lax.optimization_barrier((value, *others))[0]


def halves_swapped(a):
    half = a.shape[-1] // 2
    return jnp.concatenate([a[..., half:], a[..., :half]], axis=-1)


def table(values, index):
    out = jnp.int32(values[-1])
    for i, v in enumerate(values[:-1]):
        out = jnp.where(index == i, jnp.int32(v), out)
    return out


def dot(a, b, out=F32):
    return jnp.dot(a, b, preferred_element_type=F32).astype(out)


def dot_tn(a, b, out=F32):
    return lax.dot_general(
        a, b, (((0,), (0,)), ((), ())), preferred_element_type=F32
    ).astype(out)


def dot_nt(a, b, out=F32):
    return lax.dot_general(
        a, b, (((1,), (1,)), ((), ())), preferred_element_type=F32
    ).astype(out)


def kdot(a, b, ca, cb):
    return lax.dot_general(a, b, (((ca,), (cb,)), ((), ())), preferred_element_type=F32)


def rms_scale(values, gain):
    return (
        values
        * lax.rsqrt(jnp.mean(values * values, axis=-1, keepdims=True) + EPSILON)
        * gain
    )


def swiglu(gate_in, up_in):
    return jax.nn.silu(gate_in) * up_in


def rope_tables(positions):
    steps = jnp.arange(HD // 2, dtype=F32)
    inverse = jnp.power(ROPE_BASE, -2.0 * steps / HD)
    angles = positions.astype(F32)[:, None] * inverse[None, :]
    cosine, sine = jnp.cos(angles), jnp.sin(angles)
    return (
        jnp.concatenate([cosine, cosine], axis=1),
        jnp.concatenate([-sine, sine], axis=1),
    )


def qkv_kernel(nq, nk, part_ref, x_ref, w_ref, cos_ref, sin_ref, q_ref, kv_ref):
    acc = part_ref[...] + kdot(x_ref[...], w_ref[...], 1, 0)
    cosine, sine = cos_ref[...], sin_ref[...]
    for h in range(nq + nk):
        u = acc[:, h * HD : (h + 1) * HD]
        r = (u * cosine + pltpu.roll(u, HD // 2, 1) * sine).astype(BF16)
        if h < nq:
            q_ref[:, h * HD : (h + 1) * HD] = r
        else:
            kv_ref[:, (h - nq) * HD : (h - nq + 1) * HD] = r
    kv_ref[:, nk * HD :] = acc[:, (nq + nk) * HD :].astype(BF16)


def qkv_call(part, x, w, cosine, sine, nq, nk):
    rows, width = part.shape
    depth = x.shape[1]
    return pl.pallas_call(
        partial(qkv_kernel, nq, nk),
        grid=(rows // BLK,),
        in_specs=[
            pl.BlockSpec((BLK, width), lambda i: (i, 0)),
            pl.BlockSpec((BLK, depth), lambda i: (i, 0)),
            pl.BlockSpec((depth, width), lambda i: (0, 0)),
            pl.BlockSpec((BLK, HD), lambda i: (i, 0)),
            pl.BlockSpec((BLK, HD), lambda i: (i, 0)),
        ],
        out_specs=[
            pl.BlockSpec((BLK, nq * HD), lambda i: (i, 0)),
            pl.BlockSpec((BLK, 2 * nk * HD), lambda i: (i, 0)),
        ],
        out_shape=[
            jax.ShapeDtypeStruct((rows, nq * HD), BF16),
            jax.ShapeDtypeStruct((rows, 2 * nk * HD), BF16),
        ],
        compiler_params=pltpu.CompilerParams(vmem_limit_bytes=VMEM_LIMIT),
        cost_estimate=pl.CostEstimate(
            flops=2 * rows * width * depth,
            bytes_accessed=rows * width * 6 + rows * depth * 2 + depth * width * 2,
            transcendentals=0,
        ),
    )(part, x, w, cosine, sine)


def attend_parts(meta_ref, block, unit, trunk, step):
    base = meta_ref[block * 8]
    rows = (lax.broadcasted_iota(jnp.int32, (2 * BLK, 1), 0) & (BLK - 1)) + base
    chunk = min(trunk, 1024)
    for j in range(trunk // chunk):
        step(j * chunk, chunk, rows)
    own_start = pl.multiple_of(meta_ref[block * 8 + 1], BLK)
    step(own_start, unit, jnp.where(meta_ref[block * 8 + 2] > 0, rows, -1))
    parent_start = pl.multiple_of(meta_ref[block * 8 + 3], BLK)
    step(parent_start, unit, jnp.where(meta_ref[block * 8 + 4] > 0, BIG, -1) + rows * 0)


def stacked(ref):
    a = ref[...]
    return jnp.concatenate([a[:, :HD], a[:, HD:]], axis=0)


def unstacked(a):
    return jnp.concatenate([a[:BLK], a[BLK:]], axis=1)


def weights_of(q2, keys, start, limit):
    scores = kdot(q2, keys, 1, 1) * SCALE
    place = lax.broadcasted_iota(jnp.int32, scores.shape, 1) + start
    return jnp.where(place <= limit, jnp.exp(scores), 0.0)


def fwd_kernel(unit, trunk, meta_ref, q_ref, k_ref, v_ref, att_ref, ctx_ref, tot_ref, acc, tot):
    q2 = stacked(q_ref)
    acc[...] = jnp.zeros_like(acc)
    tot[...] = jnp.zeros_like(tot)

    def step(start, size, limit):
        e = weights_of(q2, k_ref[pl.ds(start, size), :], start, limit)
        tot[...] += jnp.sum(e, axis=1, keepdims=True)
        acc[...] += kdot(e.astype(BF16), v_ref[pl.ds(start, size), :], 1, 0)

    attend_parts(meta_ref, pl.program_id(1), unit, trunk, step)
    total = jnp.broadcast_to(tot[...], acc.shape)
    context = unstacked(acc[...] / total)
    ctx_ref[...] = context
    att_ref[...] = context.astype(BF16)
    tot_ref[...] = unstacked(total)


def fwd_call(meta, q, kv, nk, unit, trunk):
    rows = q.shape[0]
    length = kv.shape[0]
    pair = 2 * HD
    tile = pl.BlockSpec((BLK, pair), lambda g, b, m: (b, g))
    return pl.pallas_call(
        partial(fwd_kernel, unit, trunk),
        grid_spec=pltpu.PrefetchScalarGridSpec(
            num_scalar_prefetch=1,
            grid=(nk, rows // BLK),
            in_specs=[
                tile,
                pl.BlockSpec((length, HD), lambda g, b, m: (0, g)),
                pl.BlockSpec((length, HD), lambda g, b, m: (0, nk + g)),
            ],
            out_specs=[tile, tile, tile],
            scratch_shapes=[pltpu.VMEM((2 * BLK, HD), F32), pltpu.VMEM((2 * BLK, 1), F32)],
        ),
        out_shape=[
            jax.ShapeDtypeStruct(q.shape, BF16),
            jax.ShapeDtypeStruct(q.shape, F32),
            jax.ShapeDtypeStruct(q.shape, F32),
        ],
        compiler_params=pltpu.CompilerParams(vmem_limit_bytes=VMEM_LIMIT),
        cost_estimate=pl.CostEstimate(
            flops=8 * rows * nk * HD * (trunk + 2 * unit),
            bytes_accessed=kv.size * 2 + q.size * 12,
            transcendentals=2 * rows * nk * (trunk + 2 * unit),
        ),
    )(meta, q, kv, kv)


def bwd_kernel(
    unit, trunk, meta_ref, q_ref, k_ref, v_ref, gc_ref, ctx_ref, tot_ref, cos_ref, sin_ref,
    dq_ref, dk_ref, dv_ref, acc,
):
    block = pl.program_id(1)

    @pl.when(block == 0)
    def _():
        dk_ref[...] = jnp.zeros_like(dk_ref)
        dv_ref[...] = jnp.zeros_like(dv_ref)

    q2 = stacked(q_ref)
    grad_context = stacked(gc_ref)
    context = stacked(ctx_ref)
    total = stacked(tot_ref)
    grad_accum = (grad_context / total).astype(BF16)
    delta = jnp.sum(grad_context * context, axis=1, keepdims=True) / total[:, :1]
    acc[...] = jnp.zeros_like(acc)

    def step(start, size, limit):
        here = pl.ds(start, size)
        keys = k_ref[here, :]
        e = weights_of(q2, keys, start, limit)
        grad_prob = kdot(grad_accum, v_ref[here, :], 1, 1)
        grad_scores = (e * (grad_prob - delta)).astype(BF16)
        acc[...] += kdot(grad_scores, keys, 1, 0)
        dk_ref[here, :] += kdot(grad_scores, q2, 0, 0)
        dv_ref[here, :] += kdot(e.astype(BF16), grad_accum, 0, 0)

    attend_parts(meta_ref, block, unit, trunk, step)
    cosine, sine = cos_ref[...], sin_ref[...]
    g = acc[...] * SCALE
    for h in range(2):
        u = g[h * BLK : (h + 1) * BLK]
        dq_ref[:, h * HD : (h + 1) * HD] = (
            u * cosine - pltpu.roll(u, HD // 2, 1) * sine
        ).astype(BF16)


def bwd_call(meta, q, kv, grad_context, context, total, cosine, sine, nk, unit, trunk):
    rows = q.shape[0]
    length = kv.shape[0]
    tile = pl.BlockSpec((BLK, 2 * HD), lambda g, b, m: (b, g))
    angle = pl.BlockSpec((BLK, HD), lambda g, b, m: (b, 0))
    head = pl.BlockSpec((length, HD), lambda g, b, m: (0, g))
    return pl.pallas_call(
        partial(bwd_kernel, unit, trunk),
        grid_spec=pltpu.PrefetchScalarGridSpec(
            num_scalar_prefetch=1,
            grid=(nk, rows // BLK),
            in_specs=[
                tile,
                head,
                pl.BlockSpec((length, HD), lambda g, b, m: (0, nk + g)),
                tile,
                tile,
                tile,
                angle,
                angle,
            ],
            out_specs=[tile, head, head],
            scratch_shapes=[pltpu.VMEM((2 * BLK, HD), F32)],
        ),
        out_shape=[
            jax.ShapeDtypeStruct(q.shape, BF16),
            jax.ShapeDtypeStruct((length, nk * HD), F32),
            jax.ShapeDtypeStruct((length, nk * HD), F32),
        ],
        compiler_params=pltpu.CompilerParams(vmem_limit_bytes=VMEM_LIMIT),
        cost_estimate=pl.CostEstimate(
            flops=20 * rows * nk * HD * (trunk + 2 * unit),
            bytes_accessed=kv.size * 6 + q.size * 16,
            transcendentals=2 * rows * nk * (trunk + 2 * unit),
        ),
    )(meta, q, kv, kv, grad_context, context, total, cosine, sine)


def dkv_kernel(nk, sum_ref, cos_ref, sin_ref, out_ref):
    cosine, sine = cos_ref[...], sin_ref[...]
    for h in range(nk):
        u = sum_ref[:, h * HD : (h + 1) * HD] * SCALE
        out_ref[:, h * HD : (h + 1) * HD] = (
            u * cosine - pltpu.roll(u, HD // 2, 1) * sine
        ).astype(BF16)
    out_ref[:, nk * HD :] = sum_ref[:, nk * HD :].astype(BF16)


def dkv_call(sums, cosine, sine, nk):
    rows, width = sums.shape
    return pl.pallas_call(
        partial(dkv_kernel, nk),
        out_shape=jax.ShapeDtypeStruct((rows, width), BF16),
        compiler_params=pltpu.CompilerParams(vmem_limit_bytes=VMEM_LIMIT),
    )(sums, cosine, sine)


def gather_ctx(a, count, c):
    if count != 4:
        return lax.all_gather(a, "ctx", axis=0, tiled=True)
    rows = a.shape[0]
    ring = [(0, 1), (1, 3), (3, 2), (2, 0)]
    origins = [c, table((2, 0, 3, 1), c), 3 - c, table((1, 3, 0, 2), c)]
    out = jnp.zeros((rows * count, a.shape[1]), a.dtype)
    for step in range(4):
        out = lax.dynamic_update_slice_in_dim(out, a, origins[step] * rows, axis=0)
        if step < 3:
            a = lax.ppermute(a, "ctx", ring)
    return out


def scatter_ctx(a, count, c):
    rows = a.shape[0] // count
    if count != 4:
        return lax.psum_scatter(a, "ctx", scatter_dimension=0, tiled=True)
    ring = [(0, 1), (1, 3), (3, 2), (2, 0)]
    owners = [table((2, 0, 3, 1), c), 3 - c, table((1, 3, 0, 2), c), c]
    carried = None
    for step in range(4):
        mine = lax.dynamic_slice_in_dim(a, owners[step] * rows, rows, axis=0)
        if carried is not None:
            mine = mine + carried.astype(F32)
        if step == 3:
            return mine
        carried = lax.ppermute(mine.astype(BF16), "ctx", ring)


class LineSum:
    def __init__(self, count, c):
        self.count = count
        self.middle = (c == 1) | (c == 2)
        self.last = [[], [], []]

    def move(self, stage, a, pairs):
        past = self.last[stage]
        if len(past) >= 2:
            a = after(a, past[-2])
        a = lax.ppermute(a, "ctx", pairs)
        past.append(a)
        return a

    def __call__(self, a):
        if self.count != 4:
            return lax.psum(a.astype(F32), "ctx")
        got = self.move(0, a, [(0, 1), (3, 2)])
        pair = (a.astype(F32) + got.astype(F32)).astype(BF16)
        got = self.move(1, pair, [(1, 2), (2, 1)])
        whole = (pair.astype(F32) + got.astype(F32)).astype(BF16)
        got = self.move(2, whole, [(1, 0), (2, 3)])
        return jnp.where(self.middle, whole, got).astype(F32)


def sum_all(a, count):
    a = a + swap_core(a)
    a = a + swap_y(a)
    a = a + swap_x(a)
    return sum_ctx(a, count)


def sum_ctx(a, count):
    step = 1
    while step < count:
        a = a + lax.ppermute(a, "ctx", [(i, i ^ step) for i in range(count)])
        step *= 2
    return a


def per_device(
    hidden_in, teacher, w_query, w_key, w_value, w_out, w_gate, w_up, w_down,
    attn_gain, ffn_gain, segment_ids, parents, positions, valid_mask,
):
    rows, width = hidden_in.shape
    half = width // 2
    quarter = rows // 4
    count = lax.axis_size("ctx")
    f, c, t = (lax.axis_index(a) for a in ("fsdp", "ctx", "tp"))
    tree_len = rows * count
    unit = tree_len // 20
    trunk = 8 * unit
    nq, nk = w_query.shape[1] // HD, w_key.shape[1] // HD
    eighth = w_gate.shape[1] // 2
    first = f == 0

    def turned(a):
        return jnp.where(first, a, halves_swapped(a))

    def reordered(a):
        cols = a.shape[1]
        a = a.reshape(2, 2, quarter, cols)
        a = jnp.where(t < 2, a, jnp.concatenate([a[1:], a[:1]], axis=0))
        a = jnp.where(t % 2 == 0, a, jnp.concatenate([a[:, 1:], a[:, :1]], axis=1))
        return a.reshape(rows, cols)

    def own_rows(a):
        return lax.dynamic_slice_in_dim(a, t * quarter, quarter, axis=0)

    def gather_tp(x):
        over_core, over_y = swap_core(x), swap_y(x)
        return [x, over_core, over_y, swap_core(over_y)]

    def gather_plane(x):
        flipped = halves_swapped(x)
        over_x, over_y, over_xy = swap_x(flipped), swap_y(x), swap_xy(flipped)
        group = jnp.concatenate([x, over_y, over_x, over_xy], axis=0)
        return jnp.concatenate([group, swap_core(group)], axis=0)

    def scatter_tp(product, a):
        cols = a.shape[1]
        blocks = a.reshape(2, 2, quarter, cols)
        sent = swap_core(product(blocks[:, 1].reshape(2 * quarter, cols)).astype(BF16))
        kept = product(blocks[:, 0].reshape(2 * quarter, cols)) + sent.astype(F32)
        over_y = swap_y(kept[quarter:].astype(BF16))
        return kept[:quarter] + over_y.astype(F32)

    def scatter_plane(product, *arrays):
        near = [a[: 4 * quarter] for a in arrays]
        far = [a[4 * quarter :] for a in arrays]
        sent = swap_core(product(*far).astype(BF16))
        kept = product(*near) + sent.astype(F32)
        to_y = kept[quarter : 2 * quarter].astype(BF16)
        to_x = halves_swapped(kept[2 * quarter : 3 * quarter].astype(BF16))
        to_xy = halves_swapped(kept[3 * quarter :].astype(BF16))
        over_xy, over_y, over_x = swap_xy(to_xy), swap_y(to_y), swap_x(to_x)
        return (
            kept[:quarter]
            + over_y.astype(F32)
            + over_x.astype(F32)
            + over_xy.astype(F32)
        )

    near_qkv = jnp.concatenate([w_query, w_key, w_value], axis=1)
    far_qkv = swap_x(near_qkv)
    far_gains = swap_x(jnp.stack([attn_gain, ffn_gain]))
    gain_attn = jnp.concatenate([attn_gain, far_gains[0]]).astype(F32)
    gain_ffn = jnp.concatenate([ffn_gain, far_gains[1]]).astype(F32)
    far_out = swap_x(after(w_out, far_qkv))
    out_full = jnp.concatenate([w_out, far_out], axis=1)

    def exchanged(w, axis, *behind):
        kept = lax.dynamic_slice_in_dim(w, f * eighth, eighth, axis=axis)
        sent = lax.dynamic_slice_in_dim(w, (1 - f) * eighth, eighth, axis=axis)
        got = swap_x(after(sent, *behind))
        return jnp.concatenate([kept, got], axis=1 - axis), got

    gate_w, got = exchanged(w_gate, 1, far_out)
    up_w, got = exchanged(w_up, 1, got)
    down_w, got = exchanged(w_down, 0, got)

    labels = jnp.arange(parents.shape[0], dtype=jnp.int32)
    seg = segment_ids[::BLK]
    parent = jnp.sum(jnp.where(seg[:, None] == labels[None, :], parents[None, :], 0), axis=1)
    grand = jnp.sum(jnp.where(parent[:, None] == labels[None, :], parents[None, :], 0), axis=1)
    all_seg = lax.all_gather(seg, "ctx", axis=0, tiled=True)
    spots = jnp.arange(all_seg.shape[0], dtype=jnp.int32)
    parent_spot = jnp.min(
        jnp.where(all_seg[None, :] == parent[:, None], spots[None, :], all_seg.shape[0] - 1),
        axis=1,
    )
    slot = c * rows + jnp.arange(seg.shape[0], dtype=jnp.int32) * BLK
    branch_or_leaf = parent >= 0
    leaf = branch_or_leaf & (grand >= 0)
    own_ok = branch_or_leaf & (valid_mask[::BLK] == 1)
    nothing = jnp.zeros_like(slot)
    meta = jnp.stack(
        [
            slot,
            jnp.where(branch_or_leaf, slot // unit * unit, 0),
            own_ok.astype(jnp.int32),
            jnp.where(leaf, parent_spot * BLK, 0),
            leaf.astype(jnp.int32),
            nothing,
            nothing,
            nothing,
        ],
        axis=1,
    ).reshape(-1)

    valid_f = valid_mask.astype(F32)
    valid_count = jnp.sum(valid_f).reshape(1, 1)
    valid_count = sum_ctx(valid_count + swap_x(valid_count), count)[0, 0]
    cosine, sine = rope_tables(positions)

    hidden = turned(hidden_in)
    normed = rms_scale(hidden.astype(F32), gain_attn).astype(BF16)
    near_normed, far_normed = normed[:, :half], normed[:, half:]
    query, kv = qkv_call(dot(near_normed, near_qkv), far_normed, far_qkv, cosine, sine, nq, nk)
    kv_all = gather_ctx(kv, count, c)
    attended, context, total = fwd_call(meta, query, kv_all, nk, unit, trunk)
    attended = reordered(attended)
    attn_out = scatter_tp(lambda a: dot(a, out_full), attended)

    hidden_own = own_rows(hidden).astype(F32)
    middle = hidden_own + attn_out
    normed_ffn = gather_plane(rms_scale(middle, gain_ffn).astype(BF16))
    gate_proj = dot(normed_ffn, gate_w)
    up_proj = dot(normed_ffn, up_w)
    activated_f, swiglu_back = jax.vjp(swiglu, gate_proj, up_proj)
    activated = activated_f.astype(BF16)
    output_f = middle + scatter_plane(lambda a: dot(a, down_w), activated)

    deviation = output_f - turned(own_rows(teacher)).astype(F32)
    valid_own = lax.dynamic_slice_in_dim(valid_f, t * quarter, quarter, axis=0)
    error_sum = jnp.sum(valid_own * jnp.mean(deviation * deviation, axis=1))
    tokens_all = rows * lax.axis_size("fsdp") * count
    loss_factor = float(width * tokens_all // 2)
    grad_output = loss_factor * 2.0 / width * valid_own[:, None] * deviation / valid_count

    line_sum = LineSum(count, c)
    grad_ffn = gather_plane(grad_output.astype(BF16))
    grad_act = dot_nt(grad_ffn, down_w)
    grad_gate_f, grad_up_f = swiglu_back(grad_act)
    grad_gate, grad_up = grad_gate_f.astype(BF16), grad_up_f.astype(BF16)

    down_sent = swap_x(dot_tn(activated, grad_ffn[:, half:], BF16))
    down_near = line_sum(dot_tn(activated, grad_ffn[:, :half], BF16))
    gate_sent = swap_x(after(dot_tn(normed_ffn[:, half:], grad_gate, BF16), down_sent))
    down_far = line_sum(down_sent)
    up_sent = swap_x(after(dot_tn(normed_ffn[:, half:], grad_up, BF16), gate_sent))
    gate_near = line_sum(dot_tn(normed_ffn[:, :half], grad_gate, BF16))
    gate_far = line_sum(gate_sent)
    up_near = line_sum(dot_tn(normed_ffn[:, :half], grad_up, BF16))
    up_far = line_sum(up_sent)

    grad_normed_ffn = scatter_plane(
        lambda a, b: dot_nt(a, gate_w) + dot_nt(b, up_w), grad_gate, grad_up
    )
    _, norm_ffn_back = jax.vjp(rms_scale, middle, gain_ffn)
    grad_middle_part, grad_ffn_gain = norm_ffn_back(grad_normed_ffn)
    grad_middle = grad_output + grad_middle_part

    grad_attn = jnp.concatenate(gather_tp(grad_middle.astype(BF16)), axis=0)
    out_sent = swap_x(dot_tn(attended, grad_attn[:, half:], BF16))
    grad_out = line_sum(
        (dot_tn(attended, grad_attn[:, :half]) + out_sent.astype(F32)).astype(BF16)
    )
    grad_context = reordered(dot_nt(grad_attn, out_full))
    grad_query, key_terms, value_terms = bwd_call(
        meta, query, kv_all, grad_context, context, total, cosine, sine, nk, unit, trunk
    )
    kv_sums = scatter_ctx(jnp.concatenate([key_terms, value_terms], axis=1), count, c)
    grad_kv = dkv_call(kv_sums, cosine, sine, nk)
    grad_qkv = jnp.concatenate([grad_query, grad_kv], axis=1)
    qkv_sent = swap_x(dot_tn(far_normed, grad_qkv, BF16))
    grad_qkv_w = line_sum(
        (dot_tn(near_normed, grad_qkv) + qkv_sent.astype(F32)).astype(BF16)
    )
    grad_normed = scatter_tp(
        lambda a: jnp.concatenate([dot_nt(a, near_qkv), dot_nt(a, far_qkv)], axis=1),
        reordered(grad_qkv),
    )
    _, norm_attn_back = jax.vjp(rms_scale, hidden_own, gain_attn)
    grad_hidden_part, grad_attn_gain = norm_attn_back(grad_normed)
    grad_hidden = grad_middle + grad_hidden_part

    def whole_rows(x, kind):
        out = jnp.zeros((rows, width), kind)
        for j, block in enumerate(gather_tp(x)):
            out = lax.dynamic_update_slice_in_dim(
                out, block.astype(kind), (t ^ j) * quarter, axis=0
            )
        return out

    def joined(near, far, axis):
        shape = list(near.shape)
        shape[axis] *= 2
        out = jnp.zeros(shape, F32)
        out = lax.dynamic_update_slice_in_dim(out, near, f * eighth, axis=axis)
        return lax.dynamic_update_slice_in_dim(out, far, (1 - f) * eighth, axis=axis)

    small = jnp.concatenate([turned(grad_attn_gain), turned(grad_ffn_gain)])
    small = jnp.concatenate([small, jnp.full((HD,), error_sum, F32)]).reshape(1, -1)
    small = sum_all(small, count)[0]
    loss_value = small[2 * width] / valid_count
    own_attn_gain = lax.dynamic_slice_in_dim(small[:width], f * half, half)
    own_ffn_gain = lax.dynamic_slice_in_dim(small[width : 2 * width], f * half, half)
    nqw, nkw = nq * HD, nk * HD
    return (
        whole_rows(turned(output_f).astype(BF16), BF16),
        loss_value,
        whole_rows(turned(grad_hidden).astype(BF16), F32),
        grad_qkv_w[:, :nqw],
        grad_qkv_w[:, nqw : nqw + nkw],
        grad_qkv_w[:, nqw + nkw :],
        grad_out,
        joined(gate_near, gate_far, 1),
        joined(up_near, up_far, 1),
        joined(down_near, down_far, 0),
        own_attn_gain,
        own_ffn_gain,
    )


def solution(mesh):
    tokens = P(("fsdp", "ctx"))
    token_rows = P(("fsdp", "ctx"), None)
    column = P("fsdp", "tp")
    row = P("tp", "fsdp")
    gain = P("fsdp")
    weights = (column, column, column, row, column, column, row, gain, gain)
    return jax.shard_map(
        per_device,
        mesh=mesh,
        in_specs=(token_rows, token_rows, *weights, tokens, P(), tokens, tokens),
        out_specs=(token_rows, P(), token_rows, *weights),
        check_vma=False,
    )
```

```python
from functools import partial
import math

import jax
import jax.numpy as jnp
from jax import lax
from jax.experimental import pallas as pl
from jax.experimental.pallas import tpu as pltpu
from jax.sharding import PartitionSpec as P

HD = 128
BLK = 128
EPSILON = 1e-05
ROPE_BASE = 1000000.0
SCALE = 1.0 / math.sqrt(HD)
F32 = jnp.float32
BF16 = jnp.bfloat16
VMEM_LIMIT = 56 * 1024 * 1024
BIG = 1 << 30


def swap_x(a):
    return lax.ppermute(a, "fsdp", [(0, 1), (1, 0)])


def swap_core(a):
    return lax.ppermute(a, "tp", [(0, 1), (1, 0), (2, 3), (3, 2)])


def swap_y(a):
    return lax.ppermute(a, "tp", [(0, 2), (2, 0), (1, 3), (3, 1)])


def swap_xy(a):
    pairs = [(f * 4 + t, (1 - f) * 4 + (t ^ 2)) for f in range(2) for t in range(4)]
    return lax.ppermute(a, ("fsdp", "tp"), pairs)


def swap_ctx(a, count, mask):
    return lax.ppermute(a, "ctx", [(i, i ^ mask) for i in range(count)])


def after(value, *others):
    return lax.optimization_barrier((value, *others))[0]


def halves_swapped(a):
    half = a.shape[-1] // 2
    return jnp.concatenate([a[..., half:], a[..., :half]], axis=-1)


def table(values, index):
    out = jnp.int32(values[-1])
    for i, v in enumerate(values[:-1]):
        out = jnp.where(index == i, jnp.int32(v), out)
    return out


def dot(a, b, out=F32):
    return jnp.dot(a, b, preferred_element_type=F32).astype(out)


def dot_tn(a, b, out=F32):
    return lax.dot_general(
        a, b, (((0,), (0,)), ((), ())), preferred_element_type=F32
    ).astype(out)


def dot_nt(a, b, out=F32):
    return lax.dot_general(
        a, b, (((1,), (1,)), ((), ())), preferred_element_type=F32
    ).astype(out)


def kdot(a, b, ca, cb):
    return lax.dot_general(a, b, (((ca,), (cb,)), ((), ())), preferred_element_type=F32)


def rms_scale(values, gain):
    return (
        values
        * lax.rsqrt(jnp.mean(values * values, axis=-1, keepdims=True) + EPSILON)
        * gain
    )


def rope_tables(positions):
    steps = jnp.arange(HD // 2, dtype=F32)
    inverse = jnp.power(ROPE_BASE, -2.0 * steps / HD)
    angles = positions.astype(F32)[:, None] * inverse[None, :]
    cosine, sine = jnp.cos(angles), jnp.sin(angles)
    return (
        jnp.concatenate([cosine, cosine], axis=1),
        jnp.concatenate([-sine, sine], axis=1),
    )


def whole(shape):
    return pl.BlockSpec(shape, lambda i: (0,) * len(shape))


def proj_kernel(turns, x_ref, cos_ref, sin_ref, *refs):
    *weights, out_ref = refs
    half = weights[0].shape[0]
    near, far = x_ref[:, :half], x_ref[:, half:]
    cosine, sine = cos_ref[...], sin_ref[...]
    at = 0
    for turn, wn, wf in zip(turns, weights[::2], weights[1::2]):
        acc = kdot(near, wn[...], 1, 0) + kdot(far, wf[...], 1, 0)
        for h in range(acc.shape[1] // HD):
            u = acc[:, h * HD : (h + 1) * HD]
            if turn:
                u = u * cosine + pltpu.roll(u, HD // 2, 1) * sine
            out_ref[:, at : at + HD] = u.astype(BF16)
            at += HD


def proj_call(x, cosine, sine, turns, weights):
    rows, width = x.shape
    size = rows // 2
    outs = sum(w.shape[1] for w in weights) // 2
    return pl.pallas_call(
        partial(proj_kernel, turns),
        grid=(2,),
        in_specs=[
            pl.BlockSpec((size, width), lambda i: (i, 0)),
            pl.BlockSpec((size, HD), lambda i: (i, 0)),
            pl.BlockSpec((size, HD), lambda i: (i, 0)),
        ]
        + [whole(w.shape) for w in weights],
        out_specs=pl.BlockSpec((size, outs), lambda i: (i, 0)),
        out_shape=jax.ShapeDtypeStruct((rows, outs), BF16),
        compiler_params=pltpu.CompilerParams(vmem_limit_bytes=VMEM_LIMIT),
    )(x, cosine, sine, *weights)


def attend_parts(meta_ref, block, unit, trunk, step):
    base = meta_ref[block * 8]
    rows = (lax.broadcasted_iota(jnp.int32, (2 * BLK, 1), 0) & (BLK - 1)) + base
    chunk = min(trunk, 1024)
    for j in range(trunk // chunk):
        step(j * chunk, chunk, rows)
    own_start = pl.multiple_of(meta_ref[block * 8 + 1], BLK)
    step(own_start, unit, jnp.where(meta_ref[block * 8 + 2] > 0, rows, -1))
    parent_start = pl.multiple_of(meta_ref[block * 8 + 3], BLK)
    step(parent_start, unit, jnp.where(meta_ref[block * 8 + 4] > 0, BIG, -1) + rows * 0)


def stacked(ref):
    a = ref[...]
    return jnp.concatenate([a[:, :HD], a[:, HD:]], axis=0)


def unstacked(a):
    return jnp.concatenate([a[:BLK], a[BLK:]], axis=1)


def weights_of(q2, keys, start, limit):
    scores = kdot(q2, keys, 1, 1) * SCALE
    place = lax.broadcasted_iota(jnp.int32, scores.shape, 1) + start
    return jnp.where(place <= limit, jnp.exp(scores), 0.0)


def fwd_kernel(unit, trunk, meta_ref, q_ref, k_ref, v_ref, att_ref, ctx_ref, tot_ref, acc, tot):
    q2 = stacked(q_ref)
    acc[...] = jnp.zeros_like(acc)
    tot[...] = jnp.zeros_like(tot)

    def step(start, size, limit):
        e = weights_of(q2, k_ref[pl.ds(start, size), :], start, limit)
        tot[...] += jnp.sum(e, axis=1, keepdims=True)
        acc[...] += kdot(e.astype(BF16), v_ref[pl.ds(start, size), :], 1, 0)

    attend_parts(meta_ref, pl.program_id(1), unit, trunk, step)
    total = jnp.broadcast_to(tot[...], acc.shape)
    context = unstacked(acc[...] / total)
    ctx_ref[...] = context
    att_ref[...] = context.astype(BF16)
    tot_ref[...] = unstacked(total)


def fwd_call(meta, q, kv, nk, unit, trunk):
    rows = q.shape[0]
    length = kv.shape[0]
    pair = 2 * HD
    tile = pl.BlockSpec((BLK, pair), lambda g, b, m: (b, g))
    return pl.pallas_call(
        partial(fwd_kernel, unit, trunk),
        grid_spec=pltpu.PrefetchScalarGridSpec(
            num_scalar_prefetch=1,
            grid=(nk, rows // BLK),
            in_specs=[
                tile,
                pl.BlockSpec((length, HD), lambda g, b, m: (0, g)),
                pl.BlockSpec((length, HD), lambda g, b, m: (0, nk + g)),
            ],
            out_specs=[tile, tile, tile],
            scratch_shapes=[pltpu.VMEM((2 * BLK, HD), F32), pltpu.VMEM((2 * BLK, 1), F32)],
        ),
        out_shape=[
            jax.ShapeDtypeStruct(q.shape, BF16),
            jax.ShapeDtypeStruct(q.shape, F32),
            jax.ShapeDtypeStruct(q.shape, F32),
        ],
        compiler_params=pltpu.CompilerParams(vmem_limit_bytes=VMEM_LIMIT),
    )(meta, q, kv, kv)


def bwd_kernel(
    unit, trunk, meta_ref, q_ref, k_ref, v_ref, gc_ref, ctx_ref, tot_ref, cos_ref, sin_ref,
    dq_ref, dk_ref, dv_ref, acc,
):
    block = pl.program_id(1)

    @pl.when(block == 0)
    def _():
        dk_ref[...] = jnp.zeros_like(dk_ref)
        dv_ref[...] = jnp.zeros_like(dv_ref)

    q2 = stacked(q_ref)
    grad_context = stacked(gc_ref)
    context = stacked(ctx_ref)
    total = stacked(tot_ref)
    grad_accum = (grad_context / total).astype(BF16)
    delta = jnp.sum(grad_context * context, axis=1, keepdims=True) / total[:, :1]
    acc[...] = jnp.zeros_like(acc)

    def step(start, size, limit):
        here = pl.ds(start, size)
        keys = k_ref[here, :]
        e = weights_of(q2, keys, start, limit)
        grad_prob = kdot(grad_accum, v_ref[here, :], 1, 1)
        grad_scores = (e * (grad_prob - delta)).astype(BF16)
        acc[...] += kdot(grad_scores, keys, 1, 0)
        dk_ref[here, :] += kdot(grad_scores, q2, 0, 0)
        dv_ref[here, :] += kdot(e.astype(BF16), grad_accum, 0, 0)

    attend_parts(meta_ref, block, unit, trunk, step)
    cosine, sine = cos_ref[...], sin_ref[...]
    g = acc[...] * SCALE
    for h in range(2):
        u = g[h * BLK : (h + 1) * BLK]
        dq_ref[:, h * HD : (h + 1) * HD] = (
            u * cosine - pltpu.roll(u, HD // 2, 1) * sine
        ).astype(BF16)


def bwd_call(meta, q, kv, grad_context, context, total, cosine, sine, nk, unit, trunk):
    rows = q.shape[0]
    length = kv.shape[0]
    tile = pl.BlockSpec((BLK, 2 * HD), lambda g, b, m: (b, g))
    angle = pl.BlockSpec((BLK, HD), lambda g, b, m: (b, 0))
    head = pl.BlockSpec((length, HD), lambda g, b, m: (0, g))
    return pl.pallas_call(
        partial(bwd_kernel, unit, trunk),
        grid_spec=pltpu.PrefetchScalarGridSpec(
            num_scalar_prefetch=1,
            grid=(nk, rows // BLK),
            in_specs=[
                tile,
                head,
                pl.BlockSpec((length, HD), lambda g, b, m: (0, nk + g)),
                tile,
                tile,
                tile,
                angle,
                angle,
            ],
            out_specs=[tile, head, head],
            scratch_shapes=[pltpu.VMEM((2 * BLK, HD), F32)],
        ),
        out_shape=[
            jax.ShapeDtypeStruct(q.shape, BF16),
            jax.ShapeDtypeStruct((length, nk * HD), F32),
            jax.ShapeDtypeStruct((length, nk * HD), F32),
        ],
        compiler_params=pltpu.CompilerParams(vmem_limit_bytes=VMEM_LIMIT),
    )(meta, q, kv, kv, grad_context, context, total, cosine, sine)


def dkv_kernel(nk, sum_ref, cos_ref, sin_ref, out_ref):
    cosine, sine = cos_ref[...], sin_ref[...]
    for h in range(nk):
        u = sum_ref[:, h * HD : (h + 1) * HD] * SCALE
        out_ref[:, h * HD : (h + 1) * HD] = (
            u * cosine - pltpu.roll(u, HD // 2, 1) * sine
        ).astype(BF16)
    out_ref[:, nk * HD :] = sum_ref[:, nk * HD :].astype(BF16)


def dkv_call(sums, cosine, sine, nk):
    rows, width = sums.shape
    return pl.pallas_call(
        partial(dkv_kernel, nk),
        out_shape=jax.ShapeDtypeStruct((rows, width), BF16),
        compiler_params=pltpu.CompilerParams(vmem_limit_bytes=VMEM_LIMIT),
    )(sums, cosine, sine)


TILE = 256


def gathered(pieces, out_ref):
    @pl.when(pl.program_id(0) == 0)
    def _():
        size = pieces[0].shape[0]
        for j, piece in enumerate(pieces):
            out_ref[j * size : (j + 1) * size, :] = piece[...]


def row_loop(rows, body):
    size = rows // 2

    @pl.loop(0, 2)
    def _(r):
        body(pl.ds(pl.multiple_of(r * size, size), size))


def up_kernel(gathers, *refs):
    n = 8 if gathers else 1
    pieces, (gn, gf, un, uf, gate_ref, up_ref, act_ref), rest = refs[:n], refs[n : n + 7], refs[n + 7 :]
    half = gn.shape[0]
    x_ref = rest[0] if gathers else pieces[0]
    if gathers:
        gathered(pieces, x_ref)

    def body(here):
        near, far = x_ref[here, :half], x_ref[here, half:]
        gate = kdot(near, gn[...], 1, 0) + kdot(far, gf[...], 1, 0)
        up = kdot(near, un[...], 1, 0) + kdot(far, uf[...], 1, 0)
        gate_ref[here, :] = gate
        up_ref[here, :] = up
        act_ref[here, :] = (gate * jax.nn.sigmoid(gate) * up).astype(BF16)

    row_loop(x_ref.shape[0], body)


def up_call(pieces, gate_near, gate_far, up_near, up_far):
    gathers = len(pieces) == 8
    size, width = pieces[0].shape
    rows = len(pieces) * size
    depth, hidden = gate_near.shape
    weight = pl.BlockSpec((depth, TILE), lambda i: (0, i))
    tile = pl.BlockSpec((rows, TILE), lambda i: (0, i))
    outs = [((rows, hidden), F32), ((rows, hidden), F32), ((rows, hidden), BF16)]
    return pl.pallas_call(
        partial(up_kernel, gathers),
        grid=(hidden // TILE,),
        in_specs=[whole((size, width))] * len(pieces) + [weight] * 4,
        out_specs=[tile, tile, tile] + ([whole((rows, width))] if gathers else []),
        out_shape=[
            jax.ShapeDtypeStruct(shape, kind)
            for shape, kind in outs + ([((rows, width), BF16)] if gathers else [])
        ],
        compiler_params=pltpu.CompilerParams(vmem_limit_bytes=VMEM_LIMIT),
    )(*pieces, gate_near, gate_far, up_near, up_far)


def act_back_kernel(gathers, *refs):
    n = 8 if gathers else 1
    pieces, (dn, df, gate_ref, up_ref, gg_ref, gu_ref), rest = refs[:n], refs[n : n + 6], refs[n + 6 :]
    half = dn.shape[1]
    x_ref = rest[0] if gathers else pieces[0]
    if gathers:
        gathered(pieces, x_ref)

    def body(here):
        grad_act = kdot(x_ref[here, :half], dn[...], 1, 1) + kdot(x_ref[here, half:], df[...], 1, 1)
        gate, up = gate_ref[here, :], up_ref[here, :]
        sg = jax.nn.sigmoid(gate)
        gg_ref[here, :] = (grad_act * up * sg * (1.0 + gate * (1.0 - sg))).astype(BF16)
        gu_ref[here, :] = (grad_act * (gate * sg)).astype(BF16)

    row_loop(x_ref.shape[0], body)


def act_back_call(pieces, down_near, down_far, gate, up):
    gathers = len(pieces) == 8
    size, width = pieces[0].shape
    rows = len(pieces) * size
    hidden, depth = down_near.shape
    weight = pl.BlockSpec((TILE, depth), lambda i: (i, 0))
    tile = pl.BlockSpec((rows, TILE), lambda i: (0, i))
    outs = [((rows, hidden), BF16), ((rows, hidden), BF16)]
    return pl.pallas_call(
        partial(act_back_kernel, gathers),
        grid=(hidden // TILE,),
        in_specs=[whole((size, width))] * len(pieces) + [weight] * 2 + [tile] * 2,
        out_specs=[tile, tile] + ([whole((rows, width))] if gathers else []),
        out_shape=[
            jax.ShapeDtypeStruct(shape, kind)
            for shape, kind in outs + ([((rows, width), BF16)] if gathers else [])
        ],
        compiler_params=pltpu.CompilerParams(vmem_limit_bytes=VMEM_LIMIT),
    )(*pieces, down_near, down_far, gate, up)


def out_kernel(count, contract, last, *refs):
    lefts, nears, fars, rest = (
        refs[:count],
        refs[count : 2 * count],
        refs[2 * count : 3 * count],
        refs[3 * count :],
    )
    i = pl.program_id(0)
    near_at = pl.ds(pl.multiple_of(i * TILE, TILE), TILE)
    width = rest[0].shape[1]
    far_at = pl.ds(pl.multiple_of(width // 2 + i * TILE, TILE), TILE)
    quarter = rest[0].shape[0] // 4

    def product(weights):
        total = kdot(lefts[0][...], weights[0][...], 1, contract)
        for left, weight in zip(lefts[1:], weights[1:]):
            total = total + kdot(left[...], weight[...], 1, contract)
        return total

    near, far = product(nears), product(fars)
    if not last:
        rest[0][:, near_at] = near.astype(BF16)
        rest[0][:, far_at] = far.astype(BF16)
        return
    sent, own_ref, y_ref, x_ref, xy_ref = rest
    near = near + sent[:, near_at].astype(F32)
    far = far + sent[:, far_at].astype(F32)
    own_ref[:, near_at] = near[:quarter]
    own_ref[:, far_at] = far[:quarter]
    near, far = near.astype(BF16), far.astype(BF16)
    y_ref[:, near_at] = near[quarter : 2 * quarter]
    y_ref[:, far_at] = far[quarter : 2 * quarter]
    x_ref[:, near_at] = far[2 * quarter : 3 * quarter]
    x_ref[:, far_at] = near[2 * quarter : 3 * quarter]
    xy_ref[:, near_at] = far[3 * quarter :]
    xy_ref[:, far_at] = near[3 * quarter :]


def out_call(lefts, nears, fars, contract, group, sent=None):
    rows = lefts[0].shape[0] // 2
    quarter = rows // 4
    depth = lefts[0].shape[1]
    half = nears[0].shape[1 - contract]
    if contract == 0:
        weight = pl.BlockSpec((depth, TILE), lambda i: (0, i))
    else:
        weight = pl.BlockSpec((TILE, depth), lambda i: (i, 0))
    n = len(lefts)
    last = sent is not None
    full = (rows, 2 * half)
    piece = (quarter, 2 * half)
    outs = [(piece, F32), (piece, BF16), (piece, BF16), (piece, BF16)] if last else [(full, BF16)]
    got = pl.pallas_call(
        partial(out_kernel, n, contract, last),
        grid=(half // TILE,),
        in_specs=[pl.BlockSpec((rows, depth), lambda i: (group, 0))] * n
        + [weight] * (2 * n)
        + ([whole(full)] if last else []),
        out_specs=[whole(shape) for shape, _ in outs],
        out_shape=[jax.ShapeDtypeStruct(shape, kind) for shape, kind in outs],
        compiler_params=pltpu.CompilerParams(vmem_limit_bytes=VMEM_LIMIT),
    )(*lefts, *nears, *fars, *((sent,) if last else ()))
    return got if last else got[0]


def all_up_kernel(first_ref, near_ref, far_ref, gn, gf, un, uf, gate_ref, up_ref, act_ref):
    near, far = near_ref[...], far_ref[...]
    gate = kdot(near, gn[...], 1, 0) + kdot(far, gf[...], 1, 0)
    up = kdot(near, un[...], 1, 0) + kdot(far, uf[...], 1, 0)
    gate_ref[...] = gate
    up_ref[...] = up
    act_ref[...] = (gate * jax.nn.sigmoid(gate) * up).astype(BF16)


def fixed(shape):
    return pl.BlockSpec(shape, lambda i, f: (0,) * len(shape))


def halves_of_rows(size, width):
    return [
        pl.BlockSpec((size, width // 2), lambda i, f: (i, f[0])),
        pl.BlockSpec((size, width // 2), lambda i, f: (i, 1 - f[0])),
    ]


def all_up_call(first, x, size, weights):
    tokens, width = x.shape
    hidden = weights[0].shape[1]
    tile = pl.BlockSpec((size, hidden), lambda i, f: (i, 0))
    return pl.pallas_call(
        all_up_kernel,
        grid_spec=pltpu.PrefetchScalarGridSpec(
            num_scalar_prefetch=1,
            grid=(tokens // size,),
            in_specs=halves_of_rows(size, width) + [fixed(w.shape) for w in weights],
            out_specs=[tile] * 3,
        ),
        out_shape=[jax.ShapeDtypeStruct((tokens, hidden), kind) for kind in (F32, F32, BF16)],
        compiler_params=pltpu.CompilerParams(vmem_limit_bytes=VMEM_LIMIT),
        cost_estimate=pl.CostEstimate(
            flops=4 * tokens * width * hidden, bytes_accessed=0, transcendentals=0
        ),
    )(first, x, x, *weights)


def put_sums(out, sum_gate, sum_up, sum_down):
    half, depth = sum_gate.shape[1], sum_gate.shape[0]
    out[:half, :] = sum_gate[...].T.astype(BF16)
    out[half : 2 * half, :] = sum_up[...].T.astype(BF16)
    down = sum_down[...].astype(BF16)
    out[2 * half : 2 * half + depth, :] = down[:, :depth]
    out[2 * half + depth :, :] = down[:, depth:]


def add_sums(sums, gg, gu, act, x, g):
    @pl.when(pl.program_id(0) == 0)
    def _():
        for total in sums:
            total[...] = jnp.zeros_like(total)

    sums[0][...] += kdot(gg, x, 0, 0)
    sums[1][...] += kdot(gu, x, 0, 0)
    sums[2][...] += kdot(act, g, 0, 0)


def far_grads_kernel(
    first_ref, xf, gn, gf, dn, df, gate_ref, up_ref, act_ref, far_ref, gg_ref, gu_ref, *sums
):
    grad_act = kdot(gn[...], dn[...], 1, 1) + kdot(gf[...], df[...], 1, 1)
    gate, up = gate_ref[...], up_ref[...]
    sg = jax.nn.sigmoid(gate)
    gg = (grad_act * up * sg * (1.0 + gate * (1.0 - sg))).astype(BF16)
    gu = (grad_act * (gate * sg)).astype(BF16)
    gg_ref[...] = gg
    gu_ref[...] = gu
    add_sums(sums, gg, gu, act_ref[...], xf[...], gf[...])

    @pl.when(pl.program_id(0) == pl.num_programs(0) - 1)
    def _():
        put_sums(far_ref, *sums)


def near_grads_kernel(first_ref, xn, gn, act_ref, gg_ref, gu_ref, near_ref, *sums):
    add_sums(sums, gg_ref[...], gu_ref[...], act_ref[...], xn[...], gn[...])

    @pl.when(pl.program_id(0) == pl.num_programs(0) - 1)
    def _():
        put_sums(near_ref, *sums)


def grads_call(kernel, first, wides, fixeds, tiles, size, outs, products):
    tokens, width = wides[0][0].shape
    half = width // 2
    depth = tiles[0].shape[1]
    assert half == 2 * depth
    near, far = halves_of_rows(size, width)
    tile = pl.BlockSpec((size, depth), lambda i, f: (i, 0))
    shape = (3 * half, depth)
    return pl.pallas_call(
        kernel,
        grid_spec=pltpu.PrefetchScalarGridSpec(
            num_scalar_prefetch=1,
            grid=(tokens // size,),
            in_specs=[near if own else far for _, own in wides]
            + [fixed(w.shape) for w in fixeds]
            + [tile] * len(tiles),
            out_specs=[fixed(shape)] + [tile] * outs,
            scratch_shapes=[pltpu.VMEM((depth, half), F32)] * 3,
        ),
        out_shape=[jax.ShapeDtypeStruct(shape, BF16)]
        + [jax.ShapeDtypeStruct((tokens, depth), BF16)] * outs,
        compiler_params=pltpu.CompilerParams(vmem_limit_bytes=VMEM_LIMIT),
        cost_estimate=products
        and pl.CostEstimate(
            flops=products * tokens * width * depth, bytes_accessed=0, transcendentals=0
        ),
    )(first, *(a for a, _ in wides), *fixeds, *tiles)


def far_grads_call(first, x, g, size, weights, forward):
    wides = [(x, False), (g, True), (g, False)]
    return grads_call(far_grads_kernel, first, wides, weights, forward, size, 2, 5)


def near_grads_call(first, x, g, size, act, back):
    wides = [(x, True), (g, True)]
    return grads_call(near_grads_kernel, first, wides, (), (act, *back), size, 0, None)[0]


def gather_ctx(a, count, c):
    if count != 4:
        return lax.all_gather(a, "ctx", axis=0, tiled=True)
    rows = a.shape[0]
    ring = [(0, 1), (1, 3), (3, 2), (2, 0)]
    origins = [c, table((2, 0, 3, 1), c), 3 - c, table((1, 3, 0, 2), c)]
    out = jnp.zeros((rows * count, a.shape[1]), a.dtype)
    for step in range(4):
        out = lax.dynamic_update_slice_in_dim(out, a, origins[step] * rows, axis=0)
        if step < 3:
            a = lax.ppermute(a, "ctx", ring)
    return out


def gather_small(a, count, c):
    out = jnp.zeros((count, a.shape[0]), a.dtype)
    out = lax.dynamic_update_slice_in_dim(out, a[None], c, axis=0)
    return sum_ctx(out, count).reshape(-1)


def scatter_ctx(a, count, c):
    rows = a.shape[0] // count
    if count != 4:
        return lax.psum_scatter(a, "ctx", scatter_dimension=0, tiled=True)
    total = lax.dynamic_slice_in_dim(a, c * rows, rows, axis=0)
    sent = [
        lax.dynamic_slice_in_dim(a, (c ^ d) * rows, rows, axis=0).astype(BF16)
        for d in (3, 2, 1)
    ]
    for d, block in zip((3, 2, 1), sent):
        total = total + swap_ctx(block, count, d).astype(F32)
    return total


def line_sum(a):
    return lax.psum(a, "ctx").astype(F32)


def sum_planes(a, count, c):
    if count != 4:
        return lax.psum(a, "ctx")
    rows = a.shape[0] // count

    def share(index):
        return lax.dynamic_slice_in_dim(a, index * rows, rows, axis=0)

    total = share(c).astype(F32)
    for d in (3, 2, 1):
        total = total + swap_ctx(share(c ^ d), count, d).astype(F32)
    total = total.astype(BF16)
    out = jnp.zeros_like(a)
    for d in (3, 2, 1, 0):
        block = swap_ctx(total, count, d) if d else total
        out = lax.dynamic_update_slice_in_dim(out, block, (c ^ d) * rows, axis=0)
    return out


def sum_all(a, count, *behind):
    a = a + swap_core(a)
    a = a + swap_y(a)
    a = sum_ctx(a, count)
    return a + swap_x(after(a, *behind))


def sum_ctx(a, count):
    step = 1
    while step < count:
        a = a + lax.ppermute(a, "ctx", [(i, i ^ step) for i in range(count)])
        step *= 2
    return a


def per_device(
    hidden_in, teacher, w_query, w_key, w_value, w_out, w_gate, w_up, w_down,
    attn_gain, ffn_gain, segment_ids, parents, positions, valid_mask,
):
    rows, width = hidden_in.shape
    half = width // 2
    quarter = rows // 4
    count = lax.axis_size("ctx")
    f, c, t = (lax.axis_index(a) for a in ("fsdp", "ctx", "tp"))
    tree_len = rows * count
    unit = tree_len // 20
    trunk = 8 * unit
    nk = w_key.shape[1] // HD
    eighth = w_gate.shape[1] // 2
    part = eighth // 2
    parity = c % 2
    first = f == 0

    def turned(a):
        return jnp.where(first, a, halves_swapped(a))

    def reordered(a):
        cols = a.shape[1]
        a = a.reshape(2, 2, quarter, cols)
        a = jnp.where(t < 2, a, jnp.concatenate([a[1:], a[:1]], axis=0))
        a = jnp.where(t % 2 == 0, a, jnp.concatenate([a[:, 1:], a[:, :1]], axis=1))
        return a.reshape(rows, cols)

    def own_rows(a):
        return lax.dynamic_slice_in_dim(a, t * quarter, quarter, axis=0)

    def gather_tp(x):
        over_core, over_y = swap_core(x), swap_y(x)
        return [x, over_core, over_y, swap_core(over_y)]

    def gather_plane(x):
        flipped = halves_swapped(x)
        group = [x, swap_y(x), swap_x(flipped), swap_xy(flipped)]
        return group + [swap_core(a) for a in group]

    def gather_all(x):
        return lax.all_gather(turned(x), ("fsdp", "ctx", "tp"), axis=0, tiled=True)

    def halves_tp(product, a):
        cols = a.shape[1]
        blocks = a.reshape(2, 2, quarter, cols)
        sent = swap_core(product(blocks[:, 1].reshape(2 * quarter, cols)).astype(BF16))
        kept = product(blocks[:, 0].reshape(2 * quarter, cols)) + sent.astype(F32)
        return kept[:quarter], kept[quarter:].astype(BF16)

    def scatter_out(lefts, nears, fars, contract):
        sent = swap_core(out_call(lefts, nears, fars, contract, 1))
        return out_call(lefts, nears, fars, contract, 0, sent)

    def scatter_sum(products, *meanwhile):
        kept, to_y, to_x, to_xy = products
        over_xy, over_y, over_x = swap_xy(to_xy), swap_y(to_y), swap_x(to_x)
        kept = after(kept, *meanwhile)
        return kept + over_y.astype(F32) + over_x.astype(F32) + over_xy.astype(F32)

    far_key, far_value = swap_x(w_key), swap_x(w_value)
    far_gains = swap_x(jnp.stack([attn_gain, ffn_gain]))
    gain_attn = jnp.concatenate([attn_gain, far_gains[0]]).astype(F32)
    gain_ffn = jnp.concatenate([ffn_gain, far_gains[1]]).astype(F32)
    far_query = swap_x(after(w_query, far_key, far_value))
    far_out = swap_x(after(w_out, far_query))

    def exchanged(w, axis, share, *behind):
        def cut(index, which):
            return lax.dynamic_slice_in_dim(w, index * eighth + which * part, part, axis=axis)

        got = swap_x(after(cut(1 - f, parity), *behind))
        if not share:
            other = swap_x(after(cut(1 - f, 1 - parity), *behind))
        else:
            other = swap_ctx(got, count, 1)
        return (cut(f, parity), got), (cut(f, 1 - parity), other)

    gate_p, gate_o = exchanged(w_gate, 1, True, far_out)
    up_p, up_o = exchanged(w_up, 1, True, gate_p[1])

    labels = jnp.arange(parents.shape[0], dtype=jnp.int32)
    seg = segment_ids[::BLK]
    parent = jnp.sum(jnp.where(seg[:, None] == labels[None, :], parents[None, :], 0), axis=1)
    grand = jnp.sum(jnp.where(parent[:, None] == labels[None, :], parents[None, :], 0), axis=1)
    all_seg = gather_small(seg, count, c)
    spots = jnp.arange(all_seg.shape[0], dtype=jnp.int32)
    parent_spot = jnp.min(
        jnp.where(all_seg[None, :] == parent[:, None], spots[None, :], all_seg.shape[0] - 1),
        axis=1,
    )
    slot = c * rows + jnp.arange(seg.shape[0], dtype=jnp.int32) * BLK
    branch_or_leaf = parent >= 0
    leaf = branch_or_leaf & (grand >= 0)
    own_ok = branch_or_leaf & (valid_mask[::BLK] == 1)
    nothing = jnp.zeros_like(slot)
    meta = jnp.stack(
        [
            slot,
            jnp.where(branch_or_leaf, slot // unit * unit, 0),
            own_ok.astype(jnp.int32),
            jnp.where(leaf, parent_spot * BLK, 0),
            leaf.astype(jnp.int32),
            nothing,
            nothing,
            nothing,
        ],
        axis=1,
    ).reshape(-1)

    valid_f = valid_mask.astype(F32)
    valid_count = jnp.sum(valid_f).reshape(1, 1)
    valid_count = sum_ctx(valid_count + swap_x(valid_count), count)[0, 0]
    cosine, sine = rope_tables(positions)

    hidden = turned(hidden_in)
    normed = rms_scale(hidden.astype(F32), gain_attn).astype(BF16)
    near_normed, far_normed = normed[:, :half], normed[:, half:]
    normed_in, meta, valid_count = lax.optimization_barrier((normed, meta, valid_count))
    kv = proj_call(
        normed_in, cosine, sine, (True, False), (w_key, far_key, w_value, far_value)
    )
    query = proj_call(after(normed_in, kv), cosine, sine, (True,), (w_query, far_query))
    kv_all = gather_ctx(kv, count, c)
    query_in, out_full = lax.optimization_barrier(
        (query, jnp.concatenate([w_out, far_out], axis=1))
    )
    attended, context, total = fwd_call(meta, query_in, kv_all, nk, unit, trunk)
    attended = after(reordered(attended), gate_p[1])
    kept, to_y = halves_tp(lambda a: dot(a, out_full), attended)
    attn_out = kept + swap_y(to_y).astype(F32)

    hidden_own = own_rows(hidden).astype(F32)
    middle = hidden_own + attn_out
    normed_own = after(rms_scale(middle, gain_ffn).astype(BF16), up_p[1], gate_o[1])
    normed_pieces = gather_plane(normed_own)
    down_p, down_o = exchanged(w_down, 0, False, normed_pieces[2])
    *act_p, normed_ffn = up_call(normed_pieces, *gate_p, *up_p)
    shares = count == 4
    normed_ffn = after(normed_ffn, down_p[1])
    act_o = list(up_call([normed_ffn], *gate_o, *up_o))
    output_f = middle + scatter_sum(
        scatter_out([act_p[2], act_o[2]], [down_p[0], down_o[0]], [down_p[1], down_o[1]], 0)
    )

    deviation = output_f - turned(own_rows(teacher)).astype(F32)
    valid_own = lax.dynamic_slice_in_dim(valid_f, t * quarter, quarter, axis=0)
    error_sum = jnp.sum(valid_own * jnp.mean(deviation * deviation, axis=1))
    tokens_all = rows * lax.axis_size("fsdp") * count
    loss_factor = float(width * tokens_all // 2)
    grad_output = loss_factor * 2.0 / width * valid_own[:, None] * deviation / valid_count

    grad_own = grad_output.astype(BF16)
    grad_pieces = gather_plane(grad_own)
    if shares:
        normed_all, grad_all = gather_all(normed_own), gather_all(grad_own)
        place = f.reshape(1)
    gg_p, gu_p, grad_ffn = act_back_call(grad_pieces, *down_p, act_p[0], act_p[1])
    gg_o, gu_o = act_back_call([grad_ffn], *down_o, act_o[0], act_o[1])
    products = scatter_out(
        [gg_p, gu_p, gg_o, gu_o],
        [gate_p[0], up_p[0], gate_o[0], up_o[0]],
        [gate_p[1], up_p[1], gate_o[1], up_o[1]],
        1,
    )
    meanwhile = ()
    if shares:
        ahead_p = all_up_call(after(place, products[0]), normed_all, rows, (*gate_p, *up_p))
        meanwhile = ahead_p
    grad_normed_ffn = scatter_sum(products, *meanwhile)

    def joined(blocks, axis):
        shape = list(blocks[0][0].shape)
        shape[axis] *= 4
        out = jnp.zeros(shape, F32)
        for block, index, which in blocks:
            out = lax.dynamic_update_slice_in_dim(
                out, block.astype(F32), index * eighth + which * part, axis=axis
            )
        return out

    _, norm_ffn_back = jax.vjp(rms_scale, middle, gain_ffn)
    grad_middle_part, grad_ffn_gain = norm_ffn_back(grad_normed_ffn)
    grad_middle = grad_output + grad_middle_part

    grad_attn = gather_tp(grad_middle.astype(BF16))
    if shares:
        ahead_o = all_up_call(after(place, grad_middle), normed_all, rows, (*gate_o, *up_o))
        grad_attn[0] = after(grad_attn[0], *ahead_o)
    grad_attn = jnp.concatenate(grad_attn, axis=0)
    out_sent = swap_x(dot_tn(attended, grad_attn[:, half:], BF16))
    out_kept = dot_tn(attended, grad_attn[:, :half])
    grad_context = reordered(dot_nt(grad_attn, out_full))
    if shares:
        grad_context, grad_all = lax.optimization_barrier((grad_context, grad_all))
    grad_query, key_terms, value_terms = bwd_call(
        meta, query, kv_all, grad_context, context, total, cosine, sine, nk, unit, trunk
    )
    def query_weights():
        sent = swap_x(dot_tn(far_normed, grad_query, BF16))
        return sent, dot_tn(near_normed, grad_query)

    query_sent, query_kept = query_weights()
    if shares:
        blocks = [[], [], []]

        def keep(near, far, which):
            for side, index in ((near, f), (far, 1 - f)):
                gate, up, down = (side[k * half : (k + 1) * half] for k in range(3))
                blocks[0].append((gate, index, which))
                blocks[1].append((up, index, which))
                down = jnp.concatenate([down[:part], down[part:]], axis=1)
                blocks[2].append((down, index, which))

        place = after(place, grad_query)
        done, *back_p = far_grads_call(place, normed_all, grad_all, rows, down_p, ahead_p)
    else:

        def ordered(a, b):
            return jnp.where(parity == 0, a, b), jnp.where(parity == 0, b, a)

        def summed(pair_p, pair_o, axis):
            blocks = []
            for which, (near, far) in enumerate(zip(*(ordered(a, b) for a, b in zip(pair_p, pair_o)))):
                blocks.append((line_sum(near), f, which))
                blocks.append((line_sum(swap_x(far)), 1 - f, which))
            return joined(blocks, axis)

        def columns(g):
            return dot_tn(normed_ffn[:, :half], g, BF16), dot_tn(normed_ffn[:, half:], g, BF16)

        def lines(a):
            return dot_tn(a, grad_ffn[:, :half], BF16), dot_tn(a, grad_ffn[:, half:], BF16)

        grad_gate_w = summed(columns(gg_p), columns(gg_o), 1)
        grad_up_w = summed(columns(gu_p), columns(gu_o), 1)
        grad_down_w = summed(lines(act_p[2]), lines(act_o[2]), 0)

    kv_sums = scatter_ctx(jnp.concatenate([key_terms, value_terms], axis=1), count, c)
    if shares:
        kv_sums = after(kv_sums, done)
    grad_kv = dkv_call(kv_sums, cosine, sine, nk)
    kv_sent = dot_tn(far_normed, grad_kv, BF16)
    kv_sent = swap_x(kv_sent)
    kv_kept = dot_tn(near_normed, grad_kv)
    out_kept = after(out_kept, grad_query)
    query_part = (query_kept + query_sent.astype(F32)).astype(BF16)
    out_part = (out_kept + out_sent.astype(F32)).astype(BF16)
    nears = jnp.concatenate([w_query, w_key, w_value], axis=1)
    fars = jnp.concatenate([far_query, far_key, far_value], axis=1)
    kept, to_y = halves_tp(
        lambda a: jnp.concatenate([dot_nt(a, nears), dot_nt(a, fars)], axis=1),
        reordered(jnp.concatenate([grad_query, grad_kv], axis=1)),
    )
    if shares:
        over_p = swap_x(after(done, query_sent))
        place = after(place, done, to_y, kv_kept, query_part, out_part)
        far, *back_o = far_grads_call(place, normed_all, grad_all, rows, down_o, ahead_o)
        over_o = swap_x(far)
        over_y = swap_y(to_y)
        over_y, place = lax.optimization_barrier((over_y, after(place, far)))
        near = near_grads_call(place, normed_all, grad_all, rows, ahead_p[2], back_p)
        first_near = near
        kv_kept, over_p, place = lax.optimization_barrier(
            (kv_kept, over_p, after(place, near))
        )
        near = near_grads_call(place, normed_all, grad_all, rows, ahead_o[2], back_o)
        keep(first_near, over_p, parity)
        keep(near, over_o, 1 - parity)
        grad_gate_w, grad_up_w, grad_down_w = (
            joined(b, axis) for b, axis in zip(blocks, (1, 1, 0))
        )
    else:
        over_y = swap_y(to_y)
    grad_query_w, grad_out_w = lax.psum((query_part, out_part), "ctx")
    grad_kv_w = sum_planes((kv_kept + kv_sent.astype(F32)).astype(BF16), count, c).astype(F32)
    grad_normed = kept + over_y.astype(F32)
    _, norm_attn_back = jax.vjp(rms_scale, hidden_own, gain_attn)
    grad_hidden_part, grad_attn_gain = norm_attn_back(grad_normed)
    grad_hidden = grad_middle + grad_hidden_part

    def whole_rows(x, kind):
        out = jnp.zeros((rows, width), kind)
        for j, block in enumerate(gather_tp(x)):
            out = lax.dynamic_update_slice_in_dim(
                out, block.astype(kind), (t ^ j) * quarter, axis=0
            )
        return out

    small = jnp.concatenate(
        [turned(grad_attn_gain), turned(grad_ffn_gain), jnp.full((HD,), error_sum, F32)]
    ).reshape(1, -1)
    small = sum_all(small, count, *((over_o,) if shares else ()))[0]
    loss_value = small[2 * width] / valid_count
    own_attn_gain = lax.dynamic_slice_in_dim(small[:width], f * half, half)
    own_ffn_gain = lax.dynamic_slice_in_dim(small[width : 2 * width], f * half, half)
    return (
        whole_rows(after(turned(output_f).astype(BF16), done if shares else grad_query), BF16),
        loss_value,
        whole_rows(turned(grad_hidden).astype(BF16), F32),
        grad_query_w.astype(F32),
        grad_kv_w[:, : nk * HD],
        grad_kv_w[:, nk * HD :],
        grad_out_w.astype(F32),
        grad_gate_w,
        grad_up_w,
        grad_down_w,
        own_attn_gain,
        own_ffn_gain,
    )


def solution(mesh):
    tokens = P(("fsdp", "ctx"))
    token_rows = P(("fsdp", "ctx"), None)
    column = P("fsdp", "tp")
    row = P("tp", "fsdp")
    gain = P("fsdp")
    weights = (column, column, column, row, column, column, row, gain, gain)
    return jax.shard_map(
        per_device,
        mesh=mesh,
        in_specs=(token_rows, token_rows, *weights, tokens, P(), tokens, tokens),
        out_specs=(token_rows, P(), token_rows, *weights),
        check_vma=False,
    )
```

```python
from functools import partial
import math

import jax
import jax.numpy as jnp
from jax import lax
from jax.experimental import pallas as pl
from jax.experimental.pallas import tpu as pltpu
from jax.sharding import PartitionSpec as P

HD = 128
BLK = 128
EPSILON = 1e-05
ROPE_BASE = 1000000.0
SCALE = 1.0 / math.sqrt(HD)
F32 = jnp.float32
BF16 = jnp.bfloat16
VMEM_LIMIT = 56 * 1024 * 1024
BIG = 1 << 30
CFG = {'farcost': 1, 'a_qfar': 1, 'a_out': 1, 'kv_q': 1, 'x_kv': 1, 'b_y': 1, 'b_q': 1, 'kv_late': 1, 'n_p': 1, 's_last': 1, 'w_near': 1, 'o_q': 1, 'o_ffn': 1, 'o_near': 1, 'ow_near': 1, 'c_all': 1, 'early': 1, 'e_after': 1, 'e_hook': 1, 'e_up': 1, 'e_go': 1, 'e_gp': 1}


def on(name, *values):
    return values if CFG.get(name) else ()


def swap_x(a):
    return lax.ppermute(a, "fsdp", [(0, 1), (1, 0)])


def swap_core(a):
    return lax.ppermute(a, "tp", [(0, 1), (1, 0), (2, 3), (3, 2)])


def swap_y(a):
    return lax.ppermute(a, "tp", [(0, 2), (2, 0), (1, 3), (3, 1)])


def swap_xy(a):
    pairs = [(f * 4 + t, (1 - f) * 4 + (t ^ 2)) for f in range(2) for t in range(4)]
    return lax.ppermute(a, ("fsdp", "tp"), pairs)


def swap_ctx(a, count, mask):
    return lax.ppermute(a, "ctx", [(i, i ^ mask) for i in range(count)])


def after(value, *others):
    return lax.optimization_barrier((value, *others))[0]


def halves_swapped(a):
    half = a.shape[-1] // 2
    return jnp.concatenate([a[..., half:], a[..., :half]], axis=-1)


def table(values, index):
    out = jnp.int32(values[-1])
    for i, v in enumerate(values[:-1]):
        out = jnp.where(index == i, jnp.int32(v), out)
    return out


def dot(a, b, out=F32):
    return jnp.dot(a, b, preferred_element_type=F32).astype(out)


def dot_tn(a, b, out=F32):
    return lax.dot_general(
        a, b, (((0,), (0,)), ((), ())), preferred_element_type=F32
    ).astype(out)


def dot_nt(a, b, out=F32):
    return lax.dot_general(
        a, b, (((1,), (1,)), ((), ())), preferred_element_type=F32
    ).astype(out)


def kdot(a, b, ca, cb):
    return lax.dot_general(a, b, (((ca,), (cb,)), ((), ())), preferred_element_type=F32)


def rms_scale(values, gain):
    return (
        values
        * lax.rsqrt(jnp.mean(values * values, axis=-1, keepdims=True) + EPSILON)
        * gain
    )


def rope_tables(positions):
    steps = jnp.arange(HD // 2, dtype=F32)
    inverse = jnp.power(ROPE_BASE, -2.0 * steps / HD)
    angles = positions.astype(F32)[:, None] * inverse[None, :]
    cosine, sine = jnp.cos(angles), jnp.sin(angles)
    return (
        jnp.concatenate([cosine, cosine], axis=1),
        jnp.concatenate([-sine, sine], axis=1),
    )


def whole(shape):
    return pl.BlockSpec(shape, lambda i: (0,) * len(shape))


def proj_kernel(turns, x_ref, cos_ref, sin_ref, *refs):
    *weights, out_ref = refs
    half = weights[0].shape[0]
    near, far = x_ref[:, :half], x_ref[:, half:]
    cosine, sine = cos_ref[...], sin_ref[...]
    at = 0
    for turn, wn, wf in zip(turns, weights[::2], weights[1::2]):
        acc = kdot(near, wn[...], 1, 0) + kdot(far, wf[...], 1, 0)
        for h in range(acc.shape[1] // HD):
            u = acc[:, h * HD : (h + 1) * HD]
            if turn:
                u = u * cosine + pltpu.roll(u, HD // 2, 1) * sine
            out_ref[:, at : at + HD] = u.astype(BF16)
            at += HD


def proj_call(x, cosine, sine, turns, weights):
    rows, width = x.shape
    size = rows // 2
    outs = sum(w.shape[1] for w in weights) // 2
    return pl.pallas_call(
        partial(proj_kernel, turns),
        grid=(2,),
        in_specs=[
            pl.BlockSpec((size, width), lambda i: (i, 0)),
            pl.BlockSpec((size, HD), lambda i: (i, 0)),
            pl.BlockSpec((size, HD), lambda i: (i, 0)),
        ]
        + [whole(w.shape) for w in weights],
        out_specs=pl.BlockSpec((size, outs), lambda i: (i, 0)),
        out_shape=jax.ShapeDtypeStruct((rows, outs), BF16),
        compiler_params=pltpu.CompilerParams(vmem_limit_bytes=VMEM_LIMIT),
    )(x, cosine, sine, *weights)


def attend_parts(meta_ref, block, unit, trunk, step):
    base = meta_ref[block * 8]
    rows = (lax.broadcasted_iota(jnp.int32, (2 * BLK, 1), 0) & (BLK - 1)) + base
    chunk = min(trunk, 1024)
    for j in range(trunk // chunk):
        step(j * chunk, chunk, rows)
    own_start = pl.multiple_of(meta_ref[block * 8 + 1], BLK)
    step(own_start, unit, jnp.where(meta_ref[block * 8 + 2] > 0, rows, -1))
    parent_start = pl.multiple_of(meta_ref[block * 8 + 3], BLK)
    step(parent_start, unit, jnp.where(meta_ref[block * 8 + 4] > 0, BIG, -1) + rows * 0)


def stacked(ref):
    a = ref[...]
    return jnp.concatenate([a[:, :HD], a[:, HD:]], axis=0)


def unstacked(a):
    return jnp.concatenate([a[:BLK], a[BLK:]], axis=1)


def weights_of(q2, keys, start, limit):
    scores = kdot(q2, keys, 1, 1) * SCALE
    place = lax.broadcasted_iota(jnp.int32, scores.shape, 1) + start
    return jnp.where(place <= limit, jnp.exp(scores), 0.0)


def fwd_kernel(unit, trunk, meta_ref, q_ref, k_ref, v_ref, att_ref, ctx_ref, tot_ref, acc, tot):
    q2 = stacked(q_ref)
    acc[...] = jnp.zeros_like(acc)
    tot[...] = jnp.zeros_like(tot)

    def step(start, size, limit):
        e = weights_of(q2, k_ref[pl.ds(start, size), :], start, limit)
        tot[...] += jnp.sum(e, axis=1, keepdims=True)
        acc[...] += kdot(e.astype(BF16), v_ref[pl.ds(start, size), :], 1, 0)

    attend_parts(meta_ref, pl.program_id(1), unit, trunk, step)
    total = jnp.broadcast_to(tot[...], acc.shape)
    context = unstacked(acc[...] / total)
    ctx_ref[...] = context
    att_ref[...] = context.astype(BF16)
    tot_ref[...] = unstacked(total)


def fwd_call(meta, q, kv, nk, unit, trunk):
    rows = q.shape[0]
    length = kv.shape[0]
    pair = 2 * HD
    tile = pl.BlockSpec((BLK, pair), lambda g, b, m: (b, g))
    return pl.pallas_call(
        partial(fwd_kernel, unit, trunk),
        grid_spec=pltpu.PrefetchScalarGridSpec(
            num_scalar_prefetch=1,
            grid=(nk, rows // BLK),
            in_specs=[
                tile,
                pl.BlockSpec((length, HD), lambda g, b, m: (0, g)),
                pl.BlockSpec((length, HD), lambda g, b, m: (0, nk + g)),
            ],
            out_specs=[tile, tile, tile],
            scratch_shapes=[pltpu.VMEM((2 * BLK, HD), F32), pltpu.VMEM((2 * BLK, 1), F32)],
        ),
        out_shape=[
            jax.ShapeDtypeStruct(q.shape, BF16),
            jax.ShapeDtypeStruct(q.shape, F32),
            jax.ShapeDtypeStruct(q.shape, F32),
        ],
        compiler_params=pltpu.CompilerParams(vmem_limit_bytes=VMEM_LIMIT),
    )(meta, q, kv, kv)


def bwd_kernel(
    unit, trunk, meta_ref, q_ref, k_ref, v_ref, gc_ref, ctx_ref, tot_ref, cos_ref, sin_ref,
    dq_ref, dk_ref, dv_ref, acc,
):
    block = pl.program_id(1)

    @pl.when(block == 0)
    def _():
        dk_ref[...] = jnp.zeros_like(dk_ref)
        dv_ref[...] = jnp.zeros_like(dv_ref)

    q2 = stacked(q_ref)
    grad_context = stacked(gc_ref)
    context = stacked(ctx_ref)
    total = stacked(tot_ref)
    grad_accum = (grad_context / total).astype(BF16)
    delta = jnp.sum(grad_context * context, axis=1, keepdims=True) / total[:, :1]
    acc[...] = jnp.zeros_like(acc)

    def step(start, size, limit):
        here = pl.ds(start, size)
        keys = k_ref[here, :]
        e = weights_of(q2, keys, start, limit)
        grad_prob = kdot(grad_accum, v_ref[here, :], 1, 1)
        grad_scores = (e * (grad_prob - delta)).astype(BF16)
        acc[...] += kdot(grad_scores, keys, 1, 0)
        dk_ref[here, :] += kdot(grad_scores, q2, 0, 0)
        dv_ref[here, :] += kdot(e.astype(BF16), grad_accum, 0, 0)

    attend_parts(meta_ref, block, unit, trunk, step)
    cosine, sine = cos_ref[...], sin_ref[...]
    g = acc[...] * SCALE
    for h in range(2):
        u = g[h * BLK : (h + 1) * BLK]
        dq_ref[:, h * HD : (h + 1) * HD] = (
            u * cosine - pltpu.roll(u, HD // 2, 1) * sine
        ).astype(BF16)


def bwd_call(meta, q, kv, grad_context, context, total, cosine, sine, nk, unit, trunk):
    rows = q.shape[0]
    length = kv.shape[0]
    tile = pl.BlockSpec((BLK, 2 * HD), lambda g, b, m: (b, g))
    angle = pl.BlockSpec((BLK, HD), lambda g, b, m: (b, 0))
    head = pl.BlockSpec((length, HD), lambda g, b, m: (0, g))
    return pl.pallas_call(
        partial(bwd_kernel, unit, trunk),
        grid_spec=pltpu.PrefetchScalarGridSpec(
            num_scalar_prefetch=1,
            grid=(nk, rows // BLK),
            in_specs=[
                tile,
                head,
                pl.BlockSpec((length, HD), lambda g, b, m: (0, nk + g)),
                tile,
                tile,
                tile,
                angle,
                angle,
            ],
            out_specs=[tile, head, head],
            scratch_shapes=[pltpu.VMEM((2 * BLK, HD), F32)],
        ),
        out_shape=[
            jax.ShapeDtypeStruct(q.shape, BF16),
            jax.ShapeDtypeStruct((length, nk * HD), F32),
            jax.ShapeDtypeStruct((length, nk * HD), F32),
        ],
        compiler_params=pltpu.CompilerParams(vmem_limit_bytes=VMEM_LIMIT),
    )(meta, q, kv, kv, grad_context, context, total, cosine, sine)


def dkv_kernel(nk, sum_ref, cos_ref, sin_ref, out_ref):
    cosine, sine = cos_ref[...], sin_ref[...]
    for h in range(nk):
        u = sum_ref[:, h * HD : (h + 1) * HD] * SCALE
        out_ref[:, h * HD : (h + 1) * HD] = (
            u * cosine - pltpu.roll(u, HD // 2, 1) * sine
        ).astype(BF16)
    out_ref[:, nk * HD :] = sum_ref[:, nk * HD :].astype(BF16)


def dkv_call(sums, cosine, sine, nk):
    rows, width = sums.shape
    return pl.pallas_call(
        partial(dkv_kernel, nk),
        out_shape=jax.ShapeDtypeStruct((rows, width), BF16),
        compiler_params=pltpu.CompilerParams(vmem_limit_bytes=VMEM_LIMIT),
    )(sums, cosine, sine)


TILE = 256


def gathered(pieces, out_ref):
    @pl.when(pl.program_id(0) == 0)
    def _():
        size = pieces[0].shape[0]
        for j, piece in enumerate(pieces):
            out_ref[j * size : (j + 1) * size, :] = piece[...]


def row_loop(rows, body):
    size = rows // 2

    @pl.loop(0, 2)
    def _(r):
        body(pl.ds(pl.multiple_of(r * size, size), size))


def up_kernel(gathers, *refs):
    n = 8 if gathers else 1
    pieces, (gn, gf, un, uf, gate_ref, up_ref, act_ref), rest = refs[:n], refs[n : n + 7], refs[n + 7 :]
    half = gn.shape[0]
    x_ref = rest[0] if gathers else pieces[0]
    if gathers:
        gathered(pieces, x_ref)

    def body(here):
        near, far = x_ref[here, :half], x_ref[here, half:]
        gate = kdot(near, gn[...], 1, 0) + kdot(far, gf[...], 1, 0)
        up = kdot(near, un[...], 1, 0) + kdot(far, uf[...], 1, 0)
        gate_ref[here, :] = gate
        up_ref[here, :] = up
        act_ref[here, :] = (gate * jax.nn.sigmoid(gate) * up).astype(BF16)

    row_loop(x_ref.shape[0], body)


def up_call(pieces, gate_near, gate_far, up_near, up_far):
    gathers = len(pieces) == 8
    size, width = pieces[0].shape
    rows = len(pieces) * size
    depth, hidden = gate_near.shape
    weight = pl.BlockSpec((depth, TILE), lambda i: (0, i))
    tile = pl.BlockSpec((rows, TILE), lambda i: (0, i))
    outs = [((rows, hidden), F32), ((rows, hidden), F32), ((rows, hidden), BF16)]
    return pl.pallas_call(
        partial(up_kernel, gathers),
        grid=(hidden // TILE,),
        in_specs=[whole((size, width))] * len(pieces) + [weight] * 4,
        out_specs=[tile, tile, tile] + ([whole((rows, width))] if gathers else []),
        out_shape=[
            jax.ShapeDtypeStruct(shape, kind)
            for shape, kind in outs + ([((rows, width), BF16)] if gathers else [])
        ],
        compiler_params=pltpu.CompilerParams(vmem_limit_bytes=VMEM_LIMIT),
    )(*pieces, gate_near, gate_far, up_near, up_far)


def act_back_kernel(gathers, *refs):
    n = 8 if gathers else 1
    pieces, (dn, df, gate_ref, up_ref, gg_ref, gu_ref), rest = refs[:n], refs[n : n + 6], refs[n + 6 :]
    half = dn.shape[1]
    x_ref = rest[0] if gathers else pieces[0]
    if gathers:
        gathered(pieces, x_ref)

    def body(here):
        grad_act = kdot(x_ref[here, :half], dn[...], 1, 1) + kdot(x_ref[here, half:], df[...], 1, 1)
        gate, up = gate_ref[here, :], up_ref[here, :]
        sg = jax.nn.sigmoid(gate)
        gg_ref[here, :] = (grad_act * up * sg * (1.0 + gate * (1.0 - sg))).astype(BF16)
        gu_ref[here, :] = (grad_act * (gate * sg)).astype(BF16)

    row_loop(x_ref.shape[0], body)


def act_back_call(pieces, down_near, down_far, gate, up):
    gathers = len(pieces) == 8
    size, width = pieces[0].shape
    rows = len(pieces) * size
    hidden, depth = down_near.shape
    weight = pl.BlockSpec((TILE, depth), lambda i: (i, 0))
    tile = pl.BlockSpec((rows, TILE), lambda i: (0, i))
    outs = [((rows, hidden), BF16), ((rows, hidden), BF16)]
    return pl.pallas_call(
        partial(act_back_kernel, gathers),
        grid=(hidden // TILE,),
        in_specs=[whole((size, width))] * len(pieces) + [weight] * 2 + [tile] * 2,
        out_specs=[tile, tile] + ([whole((rows, width))] if gathers else []),
        out_shape=[
            jax.ShapeDtypeStruct(shape, kind)
            for shape, kind in outs + ([((rows, width), BF16)] if gathers else [])
        ],
        compiler_params=pltpu.CompilerParams(vmem_limit_bytes=VMEM_LIMIT),
    )(*pieces, down_near, down_far, gate, up)


def out_kernel(count, contract, last, *refs):
    lefts, nears, fars, rest = (
        refs[:count],
        refs[count : 2 * count],
        refs[2 * count : 3 * count],
        refs[3 * count :],
    )
    i = pl.program_id(0)
    near_at = pl.ds(pl.multiple_of(i * TILE, TILE), TILE)
    width = rest[0].shape[1]
    far_at = pl.ds(pl.multiple_of(width // 2 + i * TILE, TILE), TILE)
    quarter = rest[0].shape[0] // 4

    def product(weights):
        total = kdot(lefts[0][...], weights[0][...], 1, contract)
        for left, weight in zip(lefts[1:], weights[1:]):
            total = total + kdot(left[...], weight[...], 1, contract)
        return total

    near, far = product(nears), product(fars)
    if not last:
        rest[0][:, near_at] = near.astype(BF16)
        rest[0][:, far_at] = far.astype(BF16)
        return
    sent, own_ref, y_ref, x_ref, xy_ref = rest
    near = near + sent[:, near_at].astype(F32)
    far = far + sent[:, far_at].astype(F32)
    own_ref[:, near_at] = near[:quarter]
    own_ref[:, far_at] = far[:quarter]
    near, far = near.astype(BF16), far.astype(BF16)
    y_ref[:, near_at] = near[quarter : 2 * quarter]
    y_ref[:, far_at] = far[quarter : 2 * quarter]
    x_ref[:, near_at] = far[2 * quarter : 3 * quarter]
    x_ref[:, far_at] = near[2 * quarter : 3 * quarter]
    xy_ref[:, near_at] = far[3 * quarter :]
    xy_ref[:, far_at] = near[3 * quarter :]


def out_call(lefts, nears, fars, contract, group, sent=None):
    rows = lefts[0].shape[0] // 2
    quarter = rows // 4
    depth = lefts[0].shape[1]
    half = nears[0].shape[1 - contract]
    if contract == 0:
        weight = pl.BlockSpec((depth, TILE), lambda i: (0, i))
    else:
        weight = pl.BlockSpec((TILE, depth), lambda i: (i, 0))
    n = len(lefts)
    last = sent is not None
    full = (rows, 2 * half)
    piece = (quarter, 2 * half)
    outs = [(piece, F32), (piece, BF16), (piece, BF16), (piece, BF16)] if last else [(full, BF16)]
    got = pl.pallas_call(
        partial(out_kernel, n, contract, last),
        grid=(half // TILE,),
        in_specs=[pl.BlockSpec((rows, depth), lambda i: (group, 0))] * n
        + [weight] * (2 * n)
        + ([whole(full)] if last else []),
        out_specs=[whole(shape) for shape, _ in outs],
        out_shape=[jax.ShapeDtypeStruct(shape, kind) for shape, kind in outs],
        compiler_params=pltpu.CompilerParams(vmem_limit_bytes=VMEM_LIMIT),
    )(*lefts, *nears, *fars, *((sent,) if last else ()))
    return got if last else got[0]


def all_up_kernel(first_ref, near_ref, far_ref, gn, gf, un, uf, gate_ref, up_ref, act_ref):
    near, far = near_ref[...], far_ref[...]
    gate = kdot(near, gn[...], 1, 0) + kdot(far, gf[...], 1, 0)
    up = kdot(near, un[...], 1, 0) + kdot(far, uf[...], 1, 0)
    gate_ref[...] = gate
    up_ref[...] = up
    act_ref[...] = (gate * jax.nn.sigmoid(gate) * up).astype(BF16)


def fixed(shape):
    return pl.BlockSpec(shape, lambda i, f: (0,) * len(shape))


def halves_of_rows(size, width):
    return [
        pl.BlockSpec((size, width // 2), lambda i, f: (i, f[0])),
        pl.BlockSpec((size, width // 2), lambda i, f: (i, 1 - f[0])),
    ]


def all_up_call(first, x, size, weights):
    tokens, width = x.shape
    hidden = weights[0].shape[1]
    tile = pl.BlockSpec((size, hidden), lambda i, f: (i, 0))
    return pl.pallas_call(
        all_up_kernel,
        grid_spec=pltpu.PrefetchScalarGridSpec(
            num_scalar_prefetch=1,
            grid=(tokens // size,),
            in_specs=halves_of_rows(size, width) + [fixed(w.shape) for w in weights],
            out_specs=[tile] * 3,
        ),
        out_shape=[jax.ShapeDtypeStruct((tokens, hidden), kind) for kind in (F32, F32, BF16)],
        compiler_params=pltpu.CompilerParams(vmem_limit_bytes=VMEM_LIMIT),
        cost_estimate=pl.CostEstimate(
            flops=4 * tokens * width * hidden, bytes_accessed=0, transcendentals=0
        )
        if CFG.get('upcost')
        else None,
    )(first, x, x, *weights)


def put_sums(out, sum_gate, sum_up, sum_down):
    half, depth = sum_gate.shape[1], sum_gate.shape[0]
    out[:half, :] = sum_gate[...].T.astype(BF16)
    out[half : 2 * half, :] = sum_up[...].T.astype(BF16)
    down = sum_down[...].astype(BF16)
    out[2 * half : 2 * half + depth, :] = down[:, :depth]
    out[2 * half + depth :, :] = down[:, depth:]


def add_sums(sums, gg, gu, act, x, g):
    @pl.when(pl.program_id(0) == 0)
    def _():
        for total in sums:
            total[...] = jnp.zeros_like(total)

    sums[0][...] += kdot(gg, x, 0, 0)
    sums[1][...] += kdot(gu, x, 0, 0)
    sums[2][...] += kdot(act, g, 0, 0)


def far_grads_kernel(
    first_ref, xf, gn, gf, dn, df, gate_ref, up_ref, act_ref, far_ref, gg_ref, gu_ref, *sums
):
    grad_act = kdot(gn[...], dn[...], 1, 1) + kdot(gf[...], df[...], 1, 1)
    gate, up = gate_ref[...], up_ref[...]
    sg = jax.nn.sigmoid(gate)
    gg = (grad_act * up * sg * (1.0 + gate * (1.0 - sg))).astype(BF16)
    gu = (grad_act * (gate * sg)).astype(BF16)
    gg_ref[...] = gg
    gu_ref[...] = gu
    add_sums(sums, gg, gu, act_ref[...], xf[...], gf[...])

    @pl.when(pl.program_id(0) == pl.num_programs(0) - 1)
    def _():
        put_sums(far_ref, *sums)


def near_grads_kernel(first_ref, xn, gn, *refs):
    tiles, outs, sums = refs[:6], refs[6:8], refs[8:]
    for k in range(2):
        act, gg, gu = (ref[...] for ref in tiles[3 * k : 3 * k + 3])
        add_sums(sums[3 * k : 3 * k + 3], gg, gu, act, xn[...], gn[...])

    @pl.when(pl.program_id(0) == pl.num_programs(0) - 1)
    def _():
        for k in range(2):
            put_sums(outs[k], *sums[3 * k : 3 * k + 3])


def grads_call(kernel, first, wides, fixeds, tiles, size, outs, products):
    tokens, width = wides[0][0].shape
    half = width // 2
    depth = tiles[0].shape[1]
    assert half == 2 * depth
    near, far = halves_of_rows(size, width)
    tile = pl.BlockSpec((size, depth), lambda i, f: (i, 0))
    shape = (3 * half, depth)
    return pl.pallas_call(
        kernel,
        grid_spec=pltpu.PrefetchScalarGridSpec(
            num_scalar_prefetch=1,
            grid=(tokens // size,),
            in_specs=[near if own else far for _, own in wides]
            + [fixed(w.shape) for w in fixeds]
            + [tile] * len(tiles),
            out_specs=[fixed(shape)] + [tile] * outs,
            scratch_shapes=[pltpu.VMEM((depth, half), F32)] * 3,
        ),
        out_shape=[jax.ShapeDtypeStruct(shape, BF16)]
        + [jax.ShapeDtypeStruct((tokens, depth), BF16)] * outs,
        compiler_params=pltpu.CompilerParams(vmem_limit_bytes=VMEM_LIMIT),
        cost_estimate=products
        and pl.CostEstimate(
            flops=products * tokens * width * depth, bytes_accessed=0, transcendentals=0
        ),
    )(first, *(a for a, _ in wides), *fixeds, *tiles)


def far_grads_call(first, x, g, size, weights, forward):
    wides = [(x, False), (g, True), (g, False)]
    return grads_call(far_grads_kernel, first, wides, weights, forward, size, 2, 5 if CFG.get('farcost') else None)


def near_grads_call(first, x, g, size, tiles):
    tokens, width = x.shape
    half = width // 2
    depth = tiles[0].shape[1]
    near, _ = halves_of_rows(size, width)
    tile = pl.BlockSpec((size, depth), lambda i, f: (i, 0))
    shape = (3 * half, depth)
    return pl.pallas_call(
        near_grads_kernel,
        grid_spec=pltpu.PrefetchScalarGridSpec(
            num_scalar_prefetch=1,
            grid=(tokens // size,),
            in_specs=[near, near] + [tile] * 6,
            out_specs=[fixed(shape)] * 2,
            scratch_shapes=[pltpu.VMEM((depth, half), F32)] * 6,
        ),
        out_shape=[jax.ShapeDtypeStruct(shape, BF16)] * 2,
        compiler_params=pltpu.CompilerParams(vmem_limit_bytes=VMEM_LIMIT),
        cost_estimate=pl.CostEstimate(
            flops=6 * tokens * width * depth, bytes_accessed=0, transcendentals=0
        )
        if CFG.get('nearcost')
        else None,
    )(first, x, g, *tiles)


def place_kernel(at_ref, gate, up, left, right, *refs):
    gate_ref, up_ref, down_ref = refs[-3:]
    size = left.shape[1]
    gate_ref[...] = gate[...].astype(F32)
    up_ref[...] = up[...].astype(F32)
    down_ref[:, :size] = left[...].astype(F32)
    down_ref[:, size:] = right[...].astype(F32)


def place_call(at, block, so_far=()):
    half, depth = block.shape[0] // 3, block.shape[1]
    tall, flat = half // 4, depth // 4
    anywhere = pl.BlockSpec(memory_space=pl.ANY)
    shapes = [(half, 4 * depth)] * 2 + [(4 * depth, half)]
    return pl.pallas_call(
        place_kernel,
        grid_spec=pltpu.PrefetchScalarGridSpec(
            num_scalar_prefetch=1,
            grid=(4,),
            in_specs=[
                pl.BlockSpec((tall, depth), lambda i, w: (i, 0)),
                pl.BlockSpec((tall, depth), lambda i, w: (4 + i, 0)),
                pl.BlockSpec((flat, depth), lambda i, w: (2 * half // flat + i, 0)),
                pl.BlockSpec((flat, depth), lambda i, w: ((2 * half + depth) // flat + i, 0)),
            ]
            + [anywhere] * len(so_far),
            out_specs=[
                pl.BlockSpec((tall, depth), lambda i, w: (i, w[0])),
                pl.BlockSpec((tall, depth), lambda i, w: (i, w[0])),
                pl.BlockSpec((flat, half), lambda i, w: (4 * w[0] + i, 0)),
            ],
        ),
        out_shape=[jax.ShapeDtypeStruct(shape, F32) for shape in shapes],
        input_output_aliases={5 + k: k for k in range(len(so_far))},
        compiler_params=pltpu.CompilerParams(vmem_limit_bytes=VMEM_LIMIT),
    )(at.reshape(1), block, block, block, block, *so_far)


def gather_ctx(a, count, c):
    if count != 4:
        return lax.all_gather(a, "ctx", axis=0, tiled=True)
    rows = a.shape[0]
    ring = [(0, 1), (1, 3), (3, 2), (2, 0)]
    origins = [c, table((2, 0, 3, 1), c), 3 - c, table((1, 3, 0, 2), c)]
    out = jnp.zeros((rows * count, a.shape[1]), a.dtype)
    for step in range(4):
        out = lax.dynamic_update_slice_in_dim(out, a, origins[step] * rows, axis=0)
        if step < 3:
            a = lax.ppermute(a, "ctx", ring)
    return out


def gather_small(a, count, c):
    out = jnp.zeros((count, a.shape[0]), a.dtype)
    out = lax.dynamic_update_slice_in_dim(out, a[None], c, axis=0)
    return sum_ctx(out, count).reshape(-1)


def scatter_ctx(a, count, c):
    rows = a.shape[0] // count
    if count != 4:
        return lax.psum_scatter(a, "ctx", scatter_dimension=0, tiled=True)
    total = lax.dynamic_slice_in_dim(a, c * rows, rows, axis=0)
    sent = [
        lax.dynamic_slice_in_dim(a, (c ^ d) * rows, rows, axis=0).astype(BF16)
        for d in (3, 2, 1)
    ]
    for d, block in zip((3, 2, 1), sent):
        total = total + swap_ctx(block, count, d).astype(F32)
    return total


def line_sum(a):
    return lax.psum(a, "ctx").astype(F32)


def share_sums(a, count, c, *meanwhile):
    rows = a.shape[0] // count

    def share(index):
        return lax.dynamic_slice_in_dim(a, index * rows, rows, axis=0)

    total = after(share(c).astype(F32), *meanwhile)
    for d in (3, 2, 1):
        total = total + swap_ctx(share(c ^ d), count, d).astype(F32)
    return total.astype(BF16)


def shares_back(total, count, c, *meanwhile):
    rows = total.shape[0]
    out = after(jnp.zeros((rows * count, total.shape[1]), total.dtype), *meanwhile)
    for d in (3, 2, 1, 0):
        block = swap_ctx(total, count, d) if d else total
        out = lax.dynamic_update_slice_in_dim(out, block, (c ^ d) * rows, axis=0)
    return out


def sum_all(a, count, *behind):
    a = a + swap_core(a)
    a = a + swap_y(a)
    a = sum_ctx(a, count)
    return a + swap_x(after(a, *behind))


def sum_ctx(a, count):
    step = 1
    while step < count:
        a = a + lax.ppermute(a, "ctx", [(i, i ^ step) for i in range(count)])
        step *= 2
    return a


def per_device(
    hidden_in, teacher, w_query, w_key, w_value, w_out, w_gate, w_up, w_down,
    attn_gain, ffn_gain, segment_ids, parents, positions, valid_mask,
):
    rows, width = hidden_in.shape
    half = width // 2
    quarter = rows // 4
    count = lax.axis_size("ctx")
    f, c, t = (lax.axis_index(a) for a in ("fsdp", "ctx", "tp"))
    tree_len = rows * count
    unit = tree_len // 20
    trunk = 8 * unit
    nk = w_key.shape[1] // HD
    eighth = w_gate.shape[1] // 2
    part = eighth // 2
    parity = c % 2
    first = f == 0

    def turned(a):
        return jnp.where(first, a, halves_swapped(a))

    def reordered(a):
        cols = a.shape[1]
        a = a.reshape(2, 2, quarter, cols)
        a = jnp.where(t < 2, a, jnp.concatenate([a[1:], a[:1]], axis=0))
        a = jnp.where(t % 2 == 0, a, jnp.concatenate([a[:, 1:], a[:, :1]], axis=1))
        return a.reshape(rows, cols)

    def own_rows(a):
        return lax.dynamic_slice_in_dim(a, t * quarter, quarter, axis=0)

    def gather_tp(x):
        over_core, over_y = swap_core(x), swap_y(x)
        return [x, over_core, over_y, swap_core(over_y)]

    def gather_plane(x):
        flipped = halves_swapped(x)
        over_x = swap_x(flipped)
        group = [x, swap_y(x), over_x, swap_y(over_x) if CFG.get('e_relay') else swap_xy(flipped)]
        return group + [swap_core(a) for a in group]

    def gather_all(x):
        return lax.all_gather(turned(x), ("fsdp", "ctx", "tp"), axis=0, tiled=True)

    def halves_tp(product, a):
        cols = a.shape[1]
        blocks = a.reshape(2, 2, quarter, cols)
        sent = swap_core(product(blocks[:, 1].reshape(2 * quarter, cols)).astype(BF16))
        kept = product(blocks[:, 0].reshape(2 * quarter, cols)) + sent.astype(F32)
        return kept[:quarter], kept[quarter:].astype(BF16)

    def scatter_out(lefts, nears, fars, contract):
        sent = swap_core(out_call(lefts, nears, fars, contract, 1))
        return out_call(lefts, nears, fars, contract, 0, sent)

    def scatter_sum(products, *meanwhile):
        kept, to_y, to_x, to_xy = products
        over_xy, over_y, over_x = swap_xy(to_xy), swap_y(to_y), swap_x(to_x)
        kept = after(kept, *meanwhile)
        return kept + over_y.astype(F32) + over_x.astype(F32) + over_xy.astype(F32)

    far_key, far_value = swap_x(w_key), swap_x(w_value)
    far_gains = swap_x(jnp.stack([attn_gain, ffn_gain]))
    gain_attn = jnp.concatenate([attn_gain, far_gains[0]]).astype(F32)
    gain_ffn = jnp.concatenate([ffn_gain, far_gains[1]]).astype(F32)
    far_query = swap_x(after(w_query, far_key, far_value))
    far_out = swap_x(after(w_out, far_query))

    sends = []

    def exchanged(w, axis, share, *behind):
        def cut(index, which):
            return lax.dynamic_slice_in_dim(w, index * eighth + which * part, part, axis=axis)

        sends.append(cut(1 - f, parity))
        got = swap_x(after(sends[-1], *behind))
        if not share:
            sends.append(cut(1 - f, 1 - parity))
            other = swap_x(after(sends[-1], *behind))
        else:
            other = swap_ctx(got, count, 1)
        return (cut(f, parity), got), (cut(f, 1 - parity), other)

    gate_p, gate_o = exchanged(w_gate, 1, True, far_out)
    up_p, up_o = exchanged(w_up, 1, True, far_out if CFG.get('e_two') else gate_p[1])

    labels = jnp.arange(parents.shape[0], dtype=jnp.int32)
    seg = segment_ids[::BLK]
    parent = jnp.sum(jnp.where(seg[:, None] == labels[None, :], parents[None, :], 0), axis=1)
    grand = jnp.sum(jnp.where(parent[:, None] == labels[None, :], parents[None, :], 0), axis=1)
    all_seg = gather_small(seg, count, c)
    spots = jnp.arange(all_seg.shape[0], dtype=jnp.int32)
    parent_spot = jnp.min(
        jnp.where(all_seg[None, :] == parent[:, None], spots[None, :], all_seg.shape[0] - 1),
        axis=1,
    )
    slot = c * rows + jnp.arange(seg.shape[0], dtype=jnp.int32) * BLK
    branch_or_leaf = parent >= 0
    leaf = branch_or_leaf & (grand >= 0)
    own_ok = branch_or_leaf & (valid_mask[::BLK] == 1)
    nothing = jnp.zeros_like(slot)
    meta = jnp.stack(
        [
            slot,
            jnp.where(branch_or_leaf, slot // unit * unit, 0),
            own_ok.astype(jnp.int32),
            jnp.where(leaf, parent_spot * BLK, 0),
            leaf.astype(jnp.int32),
            nothing,
            nothing,
            nothing,
        ],
        axis=1,
    ).reshape(-1)

    valid_f = valid_mask.astype(F32)
    valid_count = jnp.sum(valid_f).reshape(1, 1)
    valid_count = sum_ctx(valid_count + swap_x(valid_count), count)[0, 0]
    cosine, sine = rope_tables(positions)

    hidden = turned(hidden_in)
    normed = rms_scale(hidden.astype(F32), gain_attn).astype(BF16)
    near_normed, far_normed = normed[:, :half], normed[:, half:]
    normed_in, meta, valid_count = lax.optimization_barrier((normed, meta, valid_count))
    normed_in = after(normed_in, *on('early', *sends))
    kv = proj_call(
        normed_in, cosine, sine, (True, False), (w_key, far_key, w_value, far_value)
    )
    query = proj_call(after(normed_in, kv), cosine, sine, (True,), (w_query, far_query))
    kv_all = gather_ctx(kv, count, c)
    query_in, out_full = lax.optimization_barrier(
        (query, jnp.concatenate([w_out, far_out], axis=1))
    )
    attended, context, total = fwd_call(meta, query_in, kv_all, nk, unit, trunk)
    attended = after(reordered(attended), *on('e_gp', gate_p[1]))
    kept, to_y = halves_tp(lambda a: dot(a, out_full), attended)
    attn_out = kept + swap_y(to_y).astype(F32)

    hidden_own = own_rows(hidden).astype(F32)
    middle = hidden_own + attn_out
    normed_own = after(rms_scale(middle, gain_ffn).astype(BF16), *on('e_up', up_p[1]), *on('e_go', gate_o[1]))
    normed_pieces = gather_plane(normed_own)
    down_p, down_o = exchanged(w_down, 0, bool(CFG.get('e_share')), *on('e_after', normed_pieces[2]), *on('e_after2', normed_pieces[3]), up_p[1])
    *act_p, normed_ffn = up_call(normed_pieces, *gate_p, *up_p)
    shares = count == 4
    normed_ffn = after(normed_ffn, *on('e_hook', down_p[1]), *on('e_hook2', up_o[1]))
    act_o = list(up_call([normed_ffn], *gate_o, *up_o))
    output_f = middle + scatter_sum(
        scatter_out([act_p[2], act_o[2]], [down_p[0], down_o[0]], [down_p[1], down_o[1]], 0)
    )

    deviation = output_f - turned(own_rows(teacher)).astype(F32)
    valid_own = lax.dynamic_slice_in_dim(valid_f, t * quarter, quarter, axis=0)
    error_sum = jnp.sum(valid_own * jnp.mean(deviation * deviation, axis=1))
    tokens_all = rows * lax.axis_size("fsdp") * count
    loss_factor = float(width * tokens_all // 2)
    grad_output = loss_factor * 2.0 / width * valid_own[:, None] * deviation / valid_count

    grad_own = grad_output.astype(BF16)
    grad_pieces = gather_plane(grad_own)
    if shares:
        normed_all, grad_all = gather_all(after(normed_own, *on('e_ag', normed_pieces[3]), *on('e_ag2', down_p[1]))), gather_all(grad_own)
        place = f.reshape(1)
    gg_p, gu_p, grad_ffn = act_back_call(grad_pieces, *down_p, act_p[0], act_p[1])
    gg_o, gu_o = act_back_call([grad_ffn], *down_o, act_o[0], act_o[1])
    products = scatter_out(
        [gg_p, gu_p, gg_o, gu_o],
        [gate_p[0], up_p[0], gate_o[0], up_o[0]],
        [gate_p[1], up_p[1], gate_o[1], up_o[1]],
        1,
    )
    meanwhile = ()
    if shares:
        ahead_p = all_up_call(after(place, products[0]), normed_all, rows, (*gate_p, *up_p))
        meanwhile = ahead_p
    grad_normed_ffn = scatter_sum(products, *meanwhile)

    def joined(blocks, axis):
        shape = list(blocks[0][0].shape)
        shape[axis] *= 4
        out = jnp.zeros(shape, F32)
        for block, index, which in blocks:
            out = lax.dynamic_update_slice_in_dim(
                out, block.astype(F32), index * eighth + which * part, axis=axis
            )
        return out

    _, norm_ffn_back = jax.vjp(rms_scale, middle, gain_ffn)
    grad_middle_part, grad_ffn_gain = norm_ffn_back(grad_normed_ffn)
    grad_middle = grad_output + grad_middle_part

    grad_attn = gather_tp(grad_middle.astype(BF16))
    if shares:
        if not CFG.get('ahead_late'):
            ahead_o = all_up_call(after(place, grad_middle), normed_all, rows, (*gate_o, *up_o))
            grad_attn[0] = after(grad_attn[0], *ahead_o)
    grad_attn = jnp.concatenate(grad_attn, axis=0)
    out_sent = swap_x(dot_tn(attended, grad_attn[:, half:], BF16))
    out_kept = dot_tn(attended, grad_attn[:, :half])
    grad_context = reordered(dot_nt(grad_attn, out_full))
    if shares and CFG.get('c_all'):
        grad_context, grad_all = lax.optimization_barrier((grad_context, grad_all))
    grad_query, key_terms, value_terms = bwd_call(
        meta, query, kv_all, grad_context, context, total, cosine, sine, nk, unit, trunk
    )
    query_far = dot_tn(far_normed, grad_query, BF16)
    query_sent, query_kept = swap_x(query_far), dot_tn(near_normed, grad_query)
    out_kept = after(out_kept, grad_query)
    out_part = (out_kept + out_sent.astype(F32)).astype(BF16)
    if shares:
        place = after(place, grad_query, *on('a_qfar', query_far), *on('a_qkept', query_kept), *on('a_out', out_part), *on('a_qsent', query_sent))
        if CFG.get('ahead_late'):
            ahead_o = all_up_call(place, normed_all, rows, (*gate_o, *up_o))
            place = after(place, *ahead_o)
        done, *back_p = far_grads_call(place, normed_all, grad_all, rows, down_p, ahead_p)
    else:

        def ordered(a, b):
            return jnp.where(parity == 0, a, b), jnp.where(parity == 0, b, a)

        def summed(pair_p, pair_o, axis):
            blocks = []
            for which, (near, far) in enumerate(zip(*(ordered(a, b) for a, b in zip(pair_p, pair_o)))):
                blocks.append((line_sum(near), f, which))
                blocks.append((line_sum(swap_x(far)), 1 - f, which))
            return joined(blocks, axis)

        def columns(g):
            return dot_tn(normed_ffn[:, :half], g, BF16), dot_tn(normed_ffn[:, half:], g, BF16)

        def lines(a):
            return dot_tn(a, grad_ffn[:, :half], BF16), dot_tn(a, grad_ffn[:, half:], BF16)

        grad_gate_w = summed(columns(gg_p), columns(gg_o), 1)
        grad_up_w = summed(columns(gu_p), columns(gu_o), 1)
        grad_down_w = summed(lines(act_p[2]), lines(act_o[2]), 0)

    kv_sums = scatter_ctx(jnp.concatenate([key_terms, value_terms], axis=1), count, c)
    if shares:
        kv_sums = after(kv_sums, done, *on('kv_q', query_sent))
    grad_kv = dkv_call(kv_sums, cosine, sine, nk)
    kv_far = dot_tn(far_normed, grad_kv, BF16)
    kv_sent, kv_kept = swap_x(kv_far), dot_tn(near_normed, grad_kv)
    query_part = (query_kept + query_sent.astype(F32)).astype(BF16)
    kv_part = None if CFG.get('kv_late') and shares else (kv_kept + kv_sent.astype(F32)).astype(BF16)
    grad_query_w, grad_out_w = lax.psum((query_part, out_part), "ctx")
    nears = jnp.concatenate([w_query, w_key, w_value], axis=1)
    fars = jnp.concatenate([far_query, far_key, far_value], axis=1)
    kept, to_y = halves_tp(
        lambda a: jnp.concatenate([dot_nt(a, nears), dot_nt(a, fars)], axis=1),
        reordered(jnp.concatenate([grad_query, grad_kv], axis=1)),
    )
    if shares:
        over_p = swap_x(after(done, *on('x_kv', kv_far), *on('x_q', query_sent)))
        place = after(place, done, *on('b_y', to_y), *on('b_q', query_part), *on('b_kv', kv_part), *on('b_kvkept', kv_kept), *on('b_out', out_part))
        far, *back_o = far_grads_call(place, normed_all, grad_all, rows, down_o, ahead_o)
        over_o = swap_x(far)
        over_y = swap_y(to_y)
        place = after(place, far)
        if CFG.get('kv_late'):
            kv_part = (after(kv_kept, far) + kv_sent.astype(F32)).astype(BF16)
            place = after(place, *on('n_kv', kv_part))
        else:
            kv_shares = share_sums(kv_part, count, c, far)
            place = after(place, *on('n_kv', kv_shares))
        place = after(place, *on('n_y', over_y), *on('n_p', over_p))
        near_p, near_o = near_grads_call(
            place, normed_all, grad_all, 2 * rows, (ahead_p[2], *back_p, ahead_o[2], *back_o)
        )
        meanwhile = (near_p,)
        weights = place_call(2 * (1 - f) + parity, over_p)
        weights = place_call(2 * f + parity, near_p, weights)
        weights = place_call(2 * f + 1 - parity, near_o, weights)
        grad_gate_w, grad_up_w, grad_down_w = place_call(
            2 * (1 - f) + 1 - parity, over_o, weights
        )
    else:
        meanwhile = ()
        over_y = swap_y(to_y)
    if shares:
        if CFG.get('kv_late'):
            kv_shares = share_sums(kv_part, count, c, *meanwhile, *on('s_ar', grad_query_w, grad_out_w))
            grad_kv_w = gather_ctx(kv_shares, count, c).astype(F32)
        else:
            grad_kv_w = shares_back(kv_shares, count, c, *meanwhile, *on('s_ar', grad_query_w, grad_out_w)).astype(F32)
    else:
        grad_kv_w = line_sum(kv_part)
    grad_normed = kept + over_y.astype(F32)
    _, norm_attn_back = jax.vjp(rms_scale, hidden_own, gain_attn)
    grad_hidden_part, grad_attn_gain = norm_attn_back(grad_normed)
    grad_hidden = after(grad_middle, *on('h_near', *meanwhile)) + grad_hidden_part

    def whole_rows(x, kind, *behind):
        pair = after(jnp.concatenate([x, swap_y(x)], axis=0), *behind)
        out = jnp.zeros((rows, width), kind)
        for k, blocks in enumerate((pair, swap_core(pair))):
            for y in range(2):
                block = blocks[y * quarter : (y + 1) * quarter].astype(kind)
                out = lax.dynamic_update_slice_in_dim(
                    out, block, (t ^ (2 * y + k)) * quarter, axis=0
                )
        return out

    small = jnp.concatenate(
        [turned(grad_attn_gain), turned(grad_ffn_gain), jnp.full((HD,), error_sum, F32)]
    ).reshape(1, -1)
    small = after(small, *on('s_near', *meanwhile))
    small = sum_all(small, count, *(on('s_last', over_o) if shares else ()))[0]
    loss_value = small[2 * width] / valid_count
    own_attn_gain = lax.dynamic_slice_in_dim(small[:width], f * half, half)
    own_ffn_gain = lax.dynamic_slice_in_dim(small[width : 2 * width], f * half, half)
    return (
        whole_rows(after(turned(output_f).astype(BF16), *on('o_q', grad_query), *on('o_ffn', grad_ffn), *(on('o_done', done) if shares else ()), *on('o_near', *meanwhile)), BF16, *on('ow_near', *meanwhile)),
        loss_value,
        whole_rows(turned(grad_hidden).astype(BF16), F32, *on('w_near', *meanwhile)),
        grad_query_w.astype(F32),
        grad_kv_w[:, : nk * HD],
        grad_kv_w[:, nk * HD :],
        grad_out_w.astype(F32),
        grad_gate_w,
        grad_up_w,
        grad_down_w,
        own_attn_gain,
        own_ffn_gain,
    )


def solution(mesh):
    tokens = P(("fsdp", "ctx"))
    token_rows = P(("fsdp", "ctx"), None)
    column = P("fsdp", "tp")
    row = P("tp", "fsdp")
    gain = P("fsdp")
    weights = (column, column, column, row, column, column, row, gain, gain)
    return jax.shard_map(
        per_device,
        mesh=mesh,
        in_specs=(token_rows, token_rows, *weights, tokens, P(), tokens, tokens),
        out_specs=(token_rows, P(), token_rows, *weights),
        check_vma=False,
    )
```

```python
from functools import partial
import math

import jax
import jax.numpy as jnp
from jax import lax
from jax.experimental import pallas as pl
from jax.experimental.pallas import tpu as pltpu
from jax.sharding import PartitionSpec as P

HD = 128
BLK = 128
EPSILON = 1e-05
ROPE_BASE = 1000000.0
SCALE = 1.0 / math.sqrt(HD)
F32 = jnp.float32
BF16 = jnp.bfloat16
VMEM_LIMIT = 56 * 1024 * 1024
BIG = 1 << 30
CFG = {'farcost': 1, 'a_qfar': 1, 'a_out': 1, 'kv_q': 1, 'x_kv': 1, 'b_y': 1, 'b_q': 1, 'kv_late': 1, 'n_p': 1, 's_last': 1, 'w_near': 1, 'o_q': 1, 'o_near': 1, 'ow_near': 1, 'c_all': 1, 'early': 1, 'e_after': 1, 'e_hook': 1, 'e_up': 1, 'e_go': 1, 'e_gp': 1, 'e_share': 1}


def on(name, *values):
    return values if CFG.get(name) else ()


def swap_x(a):
    return lax.ppermute(a, "fsdp", [(0, 1), (1, 0)])


def swap_core(a):
    return lax.ppermute(a, "tp", [(0, 1), (1, 0), (2, 3), (3, 2)])


def swap_y(a):
    return lax.ppermute(a, "tp", [(0, 2), (2, 0), (1, 3), (3, 1)])


def swap_xy(a):
    pairs = [(f * 4 + t, (1 - f) * 4 + (t ^ 2)) for f in range(2) for t in range(4)]
    return lax.ppermute(a, ("fsdp", "tp"), pairs)


def swap_ctx(a, count, mask):
    return lax.ppermute(a, "ctx", [(i, i ^ mask) for i in range(count)])


def after(value, *others):
    return lax.optimization_barrier((value, *others))[0]


def halves_swapped(a):
    half = a.shape[-1] // 2
    return jnp.concatenate([a[..., half:], a[..., :half]], axis=-1)


def table(values, index):
    out = jnp.int32(values[-1])
    for i, v in enumerate(values[:-1]):
        out = jnp.where(index == i, jnp.int32(v), out)
    return out


def dot(a, b, out=F32):
    return jnp.dot(a, b, preferred_element_type=F32).astype(out)


def dot_tn(a, b, out=F32):
    return lax.dot_general(
        a, b, (((0,), (0,)), ((), ())), preferred_element_type=F32
    ).astype(out)


def dot_nt(a, b, out=F32):
    return lax.dot_general(
        a, b, (((1,), (1,)), ((), ())), preferred_element_type=F32
    ).astype(out)


def kdot(a, b, ca, cb):
    return lax.dot_general(a, b, (((ca,), (cb,)), ((), ())), preferred_element_type=F32)


def rms_scale(values, gain):
    return (
        values
        * lax.rsqrt(jnp.mean(values * values, axis=-1, keepdims=True) + EPSILON)
        * gain
    )


def rope_tables(positions):
    steps = jnp.arange(HD // 2, dtype=F32)
    inverse = jnp.power(ROPE_BASE, -2.0 * steps / HD)
    angles = positions.astype(F32)[:, None] * inverse[None, :]
    cosine, sine = jnp.cos(angles), jnp.sin(angles)
    return (
        jnp.concatenate([cosine, cosine], axis=1),
        jnp.concatenate([-sine, sine], axis=1),
    )


def whole(shape):
    return pl.BlockSpec(shape, lambda i: (0,) * len(shape))


def proj_kernel(turns, x_ref, cos_ref, sin_ref, *refs):
    *weights, out_ref = refs
    half = weights[0].shape[0]
    near, far = x_ref[:, :half], x_ref[:, half:]
    cosine, sine = cos_ref[...], sin_ref[...]
    at = 0
    for turn, wn, wf in zip(turns, weights[::2], weights[1::2]):
        acc = kdot(near, wn[...], 1, 0) + kdot(far, wf[...], 1, 0)
        for h in range(acc.shape[1] // HD):
            u = acc[:, h * HD : (h + 1) * HD]
            if turn:
                u = u * cosine + pltpu.roll(u, HD // 2, 1) * sine
            out_ref[:, at : at + HD] = u.astype(BF16)
            at += HD


def proj_call(x, cosine, sine, turns, weights):
    rows, width = x.shape
    size = rows // 2
    outs = sum(w.shape[1] for w in weights) // 2
    return pl.pallas_call(
        partial(proj_kernel, turns),
        grid=(2,),
        in_specs=[
            pl.BlockSpec((size, width), lambda i: (i, 0)),
            pl.BlockSpec((size, HD), lambda i: (i, 0)),
            pl.BlockSpec((size, HD), lambda i: (i, 0)),
        ]
        + [whole(w.shape) for w in weights],
        out_specs=pl.BlockSpec((size, outs), lambda i: (i, 0)),
        out_shape=jax.ShapeDtypeStruct((rows, outs), BF16),
        compiler_params=pltpu.CompilerParams(vmem_limit_bytes=VMEM_LIMIT),
    )(x, cosine, sine, *weights)


def attend_parts(meta_ref, block, unit, trunk, step):
    base = meta_ref[block * 8]
    rows = (lax.broadcasted_iota(jnp.int32, (2 * BLK, 1), 0) & (BLK - 1)) + base
    chunk = min(trunk, 1024)
    for j in range(trunk // chunk):
        step(j * chunk, chunk, rows)
    own_start = pl.multiple_of(meta_ref[block * 8 + 1], BLK)
    step(own_start, unit, jnp.where(meta_ref[block * 8 + 2] > 0, rows, -1))
    parent_start = pl.multiple_of(meta_ref[block * 8 + 3], BLK)
    step(parent_start, unit, jnp.where(meta_ref[block * 8 + 4] > 0, BIG, -1) + rows * 0)


def stacked(ref):
    a = ref[...]
    return jnp.concatenate([a[:, :HD], a[:, HD:]], axis=0)


def unstacked(a):
    return jnp.concatenate([a[:BLK], a[BLK:]], axis=1)


def weights_of(q2, keys, start, limit):
    scores = kdot(q2, keys, 1, 1) * SCALE
    place = lax.broadcasted_iota(jnp.int32, scores.shape, 1) + start
    return jnp.where(place <= limit, jnp.exp(scores), 0.0)


def fwd_kernel(unit, trunk, meta_ref, q_ref, k_ref, v_ref, att_ref, ctx_ref, tot_ref, acc, tot):
    q2 = stacked(q_ref)
    acc[...] = jnp.zeros_like(acc)
    tot[...] = jnp.zeros_like(tot)

    def step(start, size, limit):
        e = weights_of(q2, k_ref[pl.ds(start, size), :], start, limit)
        tot[...] += jnp.sum(e, axis=1, keepdims=True)
        acc[...] += kdot(e.astype(BF16), v_ref[pl.ds(start, size), :], 1, 0)

    attend_parts(meta_ref, pl.program_id(1), unit, trunk, step)
    total = jnp.broadcast_to(tot[...], acc.shape)
    context = unstacked(acc[...] / total)
    ctx_ref[...] = context
    att_ref[...] = context.astype(BF16)
    tot_ref[...] = unstacked(total)


def fwd_call(meta, q, kv, nk, unit, trunk):
    rows = q.shape[0]
    length = kv.shape[0]
    pair = 2 * HD
    tile = pl.BlockSpec((BLK, pair), lambda g, b, m: (b, g))
    return pl.pallas_call(
        partial(fwd_kernel, unit, trunk),
        grid_spec=pltpu.PrefetchScalarGridSpec(
            num_scalar_prefetch=1,
            grid=(nk, rows // BLK),
            in_specs=[
                tile,
                pl.BlockSpec((length, HD), lambda g, b, m: (0, g)),
                pl.BlockSpec((length, HD), lambda g, b, m: (0, nk + g)),
            ],
            out_specs=[tile, tile, tile],
            scratch_shapes=[pltpu.VMEM((2 * BLK, HD), F32), pltpu.VMEM((2 * BLK, 1), F32)],
        ),
        out_shape=[
            jax.ShapeDtypeStruct(q.shape, BF16),
            jax.ShapeDtypeStruct(q.shape, F32),
            jax.ShapeDtypeStruct(q.shape, F32),
        ],
        compiler_params=pltpu.CompilerParams(vmem_limit_bytes=VMEM_LIMIT),
    )(meta, q, kv, kv)


def bwd_kernel(
    unit, trunk, meta_ref, q_ref, k_ref, v_ref, gc_ref, ctx_ref, tot_ref, cos_ref, sin_ref,
    dq_ref, dk_ref, dv_ref, acc,
):
    block = pl.program_id(1)

    @pl.when(block == 0)
    def _():
        dk_ref[...] = jnp.zeros_like(dk_ref)
        dv_ref[...] = jnp.zeros_like(dv_ref)

    q2 = stacked(q_ref)
    grad_context = stacked(gc_ref)
    context = stacked(ctx_ref)
    total = stacked(tot_ref)
    grad_accum = (grad_context / total).astype(BF16)
    delta = jnp.sum(grad_context * context, axis=1, keepdims=True) / total[:, :1]
    acc[...] = jnp.zeros_like(acc)

    def step(start, size, limit):
        here = pl.ds(start, size)
        keys = k_ref[here, :]
        e = weights_of(q2, keys, start, limit)
        grad_prob = kdot(grad_accum, v_ref[here, :], 1, 1)
        grad_scores = (e * (grad_prob - delta)).astype(BF16)
        acc[...] += kdot(grad_scores, keys, 1, 0)
        dk_ref[here, :] += kdot(grad_scores, q2, 0, 0)
        dv_ref[here, :] += kdot(e.astype(BF16), grad_accum, 0, 0)

    attend_parts(meta_ref, block, unit, trunk, step)
    cosine, sine = cos_ref[...], sin_ref[...]
    g = acc[...] * SCALE
    for h in range(2):
        u = g[h * BLK : (h + 1) * BLK]
        dq_ref[:, h * HD : (h + 1) * HD] = (
            u * cosine - pltpu.roll(u, HD // 2, 1) * sine
        ).astype(BF16)


def bwd_call(meta, q, kv, grad_context, context, total, cosine, sine, nk, unit, trunk):
    rows = q.shape[0]
    length = kv.shape[0]
    tile = pl.BlockSpec((BLK, 2 * HD), lambda g, b, m: (b, g))
    angle = pl.BlockSpec((BLK, HD), lambda g, b, m: (b, 0))
    head = pl.BlockSpec((length, HD), lambda g, b, m: (0, g))
    return pl.pallas_call(
        partial(bwd_kernel, unit, trunk),
        grid_spec=pltpu.PrefetchScalarGridSpec(
            num_scalar_prefetch=1,
            grid=(nk, rows // BLK),
            in_specs=[
                tile,
                head,
                pl.BlockSpec((length, HD), lambda g, b, m: (0, nk + g)),
                tile,
                tile,
                tile,
                angle,
                angle,
            ],
            out_specs=[tile, head, head],
            scratch_shapes=[pltpu.VMEM((2 * BLK, HD), F32)],
        ),
        out_shape=[
            jax.ShapeDtypeStruct(q.shape, BF16),
            jax.ShapeDtypeStruct((length, nk * HD), F32),
            jax.ShapeDtypeStruct((length, nk * HD), F32),
        ],
        compiler_params=pltpu.CompilerParams(vmem_limit_bytes=VMEM_LIMIT),
    )(meta, q, kv, kv, grad_context, context, total, cosine, sine)


def dkv_kernel(nk, sum_ref, cos_ref, sin_ref, out_ref):
    cosine, sine = cos_ref[...], sin_ref[...]
    for h in range(nk):
        u = sum_ref[:, h * HD : (h + 1) * HD] * SCALE
        out_ref[:, h * HD : (h + 1) * HD] = (
            u * cosine - pltpu.roll(u, HD // 2, 1) * sine
        ).astype(BF16)
    out_ref[:, nk * HD :] = sum_ref[:, nk * HD :].astype(BF16)


def dkv_call(sums, cosine, sine, nk):
    rows, width = sums.shape
    return pl.pallas_call(
        partial(dkv_kernel, nk),
        out_shape=jax.ShapeDtypeStruct((rows, width), BF16),
        compiler_params=pltpu.CompilerParams(vmem_limit_bytes=VMEM_LIMIT),
    )(sums, cosine, sine)


TILE = 256


def gathered(pieces, out_ref):
    @pl.when(pl.program_id(0) == 0)
    def _():
        size = pieces[0].shape[0]
        for j, piece in enumerate(pieces):
            out_ref[j * size : (j + 1) * size, :] = piece[...]


def row_loop(rows, body):
    size = rows // 2

    @pl.loop(0, 2)
    def _(r):
        body(pl.ds(pl.multiple_of(r * size, size), size))


def up_kernel(gathers, *refs):
    n = 8 if gathers else 1
    pieces, (gn, gf, un, uf, gate_ref, up_ref, act_ref), rest = refs[:n], refs[n : n + 7], refs[n + 7 :]
    half = gn.shape[0]
    x_ref = rest[0] if gathers else pieces[0]
    if gathers:
        gathered(pieces, x_ref)

    def body(here):
        near, far = x_ref[here, :half], x_ref[here, half:]
        gate = kdot(near, gn[...], 1, 0) + kdot(far, gf[...], 1, 0)
        up = kdot(near, un[...], 1, 0) + kdot(far, uf[...], 1, 0)
        gate_ref[here, :] = gate
        up_ref[here, :] = up
        act_ref[here, :] = (gate * jax.nn.sigmoid(gate) * up).astype(BF16)

    row_loop(x_ref.shape[0], body)


def up_call(pieces, gate_near, gate_far, up_near, up_far):
    gathers = len(pieces) == 8
    size, width = pieces[0].shape
    rows = len(pieces) * size
    depth, hidden = gate_near.shape
    weight = pl.BlockSpec((depth, TILE), lambda i: (0, i))
    tile = pl.BlockSpec((rows, TILE), lambda i: (0, i))
    outs = [((rows, hidden), F32), ((rows, hidden), F32), ((rows, hidden), BF16)]
    return pl.pallas_call(
        partial(up_kernel, gathers),
        grid=(hidden // TILE,),
        in_specs=[whole((size, width))] * len(pieces) + [weight] * 4,
        out_specs=[tile, tile, tile] + ([whole((rows, width))] if gathers else []),
        out_shape=[
            jax.ShapeDtypeStruct(shape, kind)
            for shape, kind in outs + ([((rows, width), BF16)] if gathers else [])
        ],
        compiler_params=pltpu.CompilerParams(vmem_limit_bytes=VMEM_LIMIT),
    )(*pieces, gate_near, gate_far, up_near, up_far)


def act_back_kernel(gathers, *refs):
    n = 8 if gathers else 1
    pieces, (dn, df, gate_ref, up_ref, gg_ref, gu_ref), rest = refs[:n], refs[n : n + 6], refs[n + 6 :]
    half = dn.shape[1]
    x_ref = rest[0] if gathers else pieces[0]
    if gathers:
        gathered(pieces, x_ref)

    def body(here):
        grad_act = kdot(x_ref[here, :half], dn[...], 1, 1) + kdot(x_ref[here, half:], df[...], 1, 1)
        gate, up = gate_ref[here, :], up_ref[here, :]
        sg = jax.nn.sigmoid(gate)
        gg_ref[here, :] = (grad_act * up * sg * (1.0 + gate * (1.0 - sg))).astype(BF16)
        gu_ref[here, :] = (grad_act * (gate * sg)).astype(BF16)

    row_loop(x_ref.shape[0], body)


def act_back_call(pieces, down_near, down_far, gate, up):
    gathers = len(pieces) == 8
    size, width = pieces[0].shape
    rows = len(pieces) * size
    hidden, depth = down_near.shape
    weight = pl.BlockSpec((TILE, depth), lambda i: (i, 0))
    tile = pl.BlockSpec((rows, TILE), lambda i: (0, i))
    outs = [((rows, hidden), BF16), ((rows, hidden), BF16)]
    return pl.pallas_call(
        partial(act_back_kernel, gathers),
        grid=(hidden // TILE,),
        in_specs=[whole((size, width))] * len(pieces) + [weight] * 2 + [tile] * 2,
        out_specs=[tile, tile] + ([whole((rows, width))] if gathers else []),
        out_shape=[
            jax.ShapeDtypeStruct(shape, kind)
            for shape, kind in outs + ([((rows, width), BF16)] if gathers else [])
        ],
        compiler_params=pltpu.CompilerParams(vmem_limit_bytes=VMEM_LIMIT),
    )(*pieces, down_near, down_far, gate, up)


def out_kernel(count, contract, last, *refs):
    lefts, nears, fars, rest = (
        refs[:count],
        refs[count : 2 * count],
        refs[2 * count : 3 * count],
        refs[3 * count :],
    )
    i = pl.program_id(0)
    near_at = pl.ds(pl.multiple_of(i * TILE, TILE), TILE)
    width = rest[0].shape[1]
    far_at = pl.ds(pl.multiple_of(width // 2 + i * TILE, TILE), TILE)
    quarter = rest[0].shape[0] // 4

    def product(weights):
        total = kdot(lefts[0][...], weights[0][...], 1, contract)
        for left, weight in zip(lefts[1:], weights[1:]):
            total = total + kdot(left[...], weight[...], 1, contract)
        return total

    near, far = product(nears), product(fars)
    if not last:
        rest[0][:, near_at] = near.astype(BF16)
        rest[0][:, far_at] = far.astype(BF16)
        return
    sent, own_ref, y_ref, x_ref, xy_ref = rest
    near = near + sent[:, near_at].astype(F32)
    far = far + sent[:, far_at].astype(F32)
    own_ref[:, near_at] = near[:quarter]
    own_ref[:, far_at] = far[:quarter]
    near, far = near.astype(BF16), far.astype(BF16)
    y_ref[:, near_at] = near[quarter : 2 * quarter]
    y_ref[:, far_at] = far[quarter : 2 * quarter]
    x_ref[:, near_at] = far[2 * quarter : 3 * quarter]
    x_ref[:, far_at] = near[2 * quarter : 3 * quarter]
    xy_ref[:, near_at] = far[3 * quarter :]
    xy_ref[:, far_at] = near[3 * quarter :]


def out_call(lefts, nears, fars, contract, group, sent=None):
    rows = lefts[0].shape[0] // 2
    quarter = rows // 4
    depth = lefts[0].shape[1]
    half = nears[0].shape[1 - contract]
    if contract == 0:
        weight = pl.BlockSpec((depth, TILE), lambda i: (0, i))
    else:
        weight = pl.BlockSpec((TILE, depth), lambda i: (i, 0))
    n = len(lefts)
    last = sent is not None
    full = (rows, 2 * half)
    piece = (quarter, 2 * half)
    outs = [(piece, F32), (piece, BF16), (piece, BF16), (piece, BF16)] if last else [(full, BF16)]
    got = pl.pallas_call(
        partial(out_kernel, n, contract, last),
        grid=(half // TILE,),
        in_specs=[pl.BlockSpec((rows, depth), lambda i: (group, 0))] * n
        + [weight] * (2 * n)
        + ([whole(full)] if last else []),
        out_specs=[whole(shape) for shape, _ in outs],
        out_shape=[jax.ShapeDtypeStruct(shape, kind) for shape, kind in outs],
        compiler_params=pltpu.CompilerParams(vmem_limit_bytes=VMEM_LIMIT),
    )(*lefts, *nears, *fars, *((sent,) if last else ()))
    return got if last else got[0]


def all_up_kernel(first_ref, near_ref, far_ref, gn, gf, un, uf, gate_ref, up_ref, act_ref):
    near, far = near_ref[...], far_ref[...]
    gate = kdot(near, gn[...], 1, 0) + kdot(far, gf[...], 1, 0)
    up = kdot(near, un[...], 1, 0) + kdot(far, uf[...], 1, 0)
    gate_ref[...] = gate
    up_ref[...] = up
    act_ref[...] = (gate * jax.nn.sigmoid(gate) * up).astype(BF16)


def fixed(shape):
    return pl.BlockSpec(shape, lambda i, f: (0,) * len(shape))


def halves_of_rows(size, width):
    return [
        pl.BlockSpec((size, width // 2), lambda i, f: (i, f[0])),
        pl.BlockSpec((size, width // 2), lambda i, f: (i, 1 - f[0])),
    ]


def all_up_call(first, x, size, weights):
    tokens, width = x.shape
    hidden = weights[0].shape[1]
    tile = pl.BlockSpec((size, hidden), lambda i, f: (i, 0))
    return pl.pallas_call(
        all_up_kernel,
        grid_spec=pltpu.PrefetchScalarGridSpec(
            num_scalar_prefetch=1,
            grid=(tokens // size,),
            in_specs=halves_of_rows(size, width) + [fixed(w.shape) for w in weights],
            out_specs=[tile] * 3,
        ),
        out_shape=[jax.ShapeDtypeStruct((tokens, hidden), kind) for kind in (F32, F32, BF16)],
        compiler_params=pltpu.CompilerParams(vmem_limit_bytes=VMEM_LIMIT),
        cost_estimate=pl.CostEstimate(
            flops=4 * tokens * width * hidden, bytes_accessed=0, transcendentals=0
        )
        if CFG.get('upcost')
        else None,
    )(first, x, x, *weights)


def put_sums(out, sum_gate, sum_up, sum_down):
    half, depth = sum_gate.shape[1], sum_gate.shape[0]
    out[:half, :] = sum_gate[...].T.astype(BF16)
    out[half : 2 * half, :] = sum_up[...].T.astype(BF16)
    down = sum_down[...].astype(BF16)
    out[2 * half : 2 * half + depth, :] = down[:, :depth]
    out[2 * half + depth :, :] = down[:, depth:]


def add_sums(sums, gg, gu, act, x, g):
    @pl.when(pl.program_id(0) == 0)
    def _():
        for total in sums:
            total[...] = jnp.zeros_like(total)

    sums[0][...] += kdot(gg, x, 0, 0)
    sums[1][...] += kdot(gu, x, 0, 0)
    sums[2][...] += kdot(act, g, 0, 0)


def far_grads_kernel(
    first_ref, xf, gn, gf, dn, df, gate_ref, up_ref, act_ref, far_ref, gg_ref, gu_ref, *sums
):
    grad_act = kdot(gn[...], dn[...], 1, 1) + kdot(gf[...], df[...], 1, 1)
    gate, up = gate_ref[...], up_ref[...]
    sg = jax.nn.sigmoid(gate)
    gg = (grad_act * up * sg * (1.0 + gate * (1.0 - sg))).astype(BF16)
    gu = (grad_act * (gate * sg)).astype(BF16)
    gg_ref[...] = gg
    gu_ref[...] = gu
    add_sums(sums, gg, gu, act_ref[...], xf[...], gf[...])

    @pl.when(pl.program_id(0) == pl.num_programs(0) - 1)
    def _():
        put_sums(far_ref, *sums)


def near_grads_kernel(first_ref, xn, gn, *refs):
    tiles, outs, sums = refs[:6], refs[6:8], refs[8:]
    for k in range(2):
        act, gg, gu = (ref[...] for ref in tiles[3 * k : 3 * k + 3])
        add_sums(sums[3 * k : 3 * k + 3], gg, gu, act, xn[...], gn[...])

    @pl.when(pl.program_id(0) == pl.num_programs(0) - 1)
    def _():
        for k in range(2):
            put_sums(outs[k], *sums[3 * k : 3 * k + 3])


def grads_call(kernel, first, wides, fixeds, tiles, size, outs, products):
    tokens, width = wides[0][0].shape
    half = width // 2
    depth = tiles[0].shape[1]
    assert half == 2 * depth
    near, far = halves_of_rows(size, width)
    tile = pl.BlockSpec((size, depth), lambda i, f: (i, 0))
    shape = (3 * half, depth)
    return pl.pallas_call(
        kernel,
        grid_spec=pltpu.PrefetchScalarGridSpec(
            num_scalar_prefetch=1,
            grid=(tokens // size,),
            in_specs=[near if own else far for _, own in wides]
            + [fixed(w.shape) for w in fixeds]
            + [tile] * len(tiles),
            out_specs=[fixed(shape)] + [tile] * outs,
            scratch_shapes=[pltpu.VMEM((depth, half), F32)] * 3,
        ),
        out_shape=[jax.ShapeDtypeStruct(shape, BF16)]
        + [jax.ShapeDtypeStruct((tokens, depth), BF16)] * outs,
        compiler_params=pltpu.CompilerParams(vmem_limit_bytes=VMEM_LIMIT),
        cost_estimate=products
        and pl.CostEstimate(
            flops=products * tokens * width * depth, bytes_accessed=0, transcendentals=0
        ),
    )(first, *(a for a, _ in wides), *fixeds, *tiles)


def far_grads_call(first, x, g, size, weights, forward):
    wides = [(x, False), (g, True), (g, False)]
    return grads_call(far_grads_kernel, first, wides, weights, forward, size, 2, 5 if CFG.get('farcost') else None)


def near_grads_call(first, x, g, size, tiles):
    tokens, width = x.shape
    half = width // 2
    depth = tiles[0].shape[1]
    near, _ = halves_of_rows(size, width)
    tile = pl.BlockSpec((size, depth), lambda i, f: (i, 0))
    shape = (3 * half, depth)
    return pl.pallas_call(
        near_grads_kernel,
        grid_spec=pltpu.PrefetchScalarGridSpec(
            num_scalar_prefetch=1,
            grid=(tokens // size,),
            in_specs=[near, near] + [tile] * 6,
            out_specs=[fixed(shape)] * 2,
            scratch_shapes=[pltpu.VMEM((depth, half), F32)] * 6,
        ),
        out_shape=[jax.ShapeDtypeStruct(shape, BF16)] * 2,
        compiler_params=pltpu.CompilerParams(vmem_limit_bytes=VMEM_LIMIT),
        cost_estimate=pl.CostEstimate(
            flops=6 * tokens * width * depth, bytes_accessed=0, transcendentals=0
        )
        if CFG.get('nearcost')
        else None,
    )(first, x, g, *tiles)


def place_kernel(at_ref, gate, up, left, right, *refs):
    gate_ref, up_ref, down_ref = refs[-3:]
    size = left.shape[1]
    gate_ref[...] = gate[...].astype(F32)
    up_ref[...] = up[...].astype(F32)
    down_ref[:, :size] = left[...].astype(F32)
    down_ref[:, size:] = right[...].astype(F32)


def place_call(at, block, so_far=()):
    half, depth = block.shape[0] // 3, block.shape[1]
    tall, flat = half // 4, depth // 4
    anywhere = pl.BlockSpec(memory_space=pl.ANY)
    shapes = [(half, 4 * depth)] * 2 + [(4 * depth, half)]
    return pl.pallas_call(
        place_kernel,
        grid_spec=pltpu.PrefetchScalarGridSpec(
            num_scalar_prefetch=1,
            grid=(4,),
            in_specs=[
                pl.BlockSpec((tall, depth), lambda i, w: (i, 0)),
                pl.BlockSpec((tall, depth), lambda i, w: (4 + i, 0)),
                pl.BlockSpec((flat, depth), lambda i, w: (2 * half // flat + i, 0)),
                pl.BlockSpec((flat, depth), lambda i, w: ((2 * half + depth) // flat + i, 0)),
            ]
            + [anywhere] * len(so_far),
            out_specs=[
                pl.BlockSpec((tall, depth), lambda i, w: (i, w[0])),
                pl.BlockSpec((tall, depth), lambda i, w: (i, w[0])),
                pl.BlockSpec((flat, half), lambda i, w: (4 * w[0] + i, 0)),
            ],
        ),
        out_shape=[jax.ShapeDtypeStruct(shape, F32) for shape in shapes],
        input_output_aliases={5 + k: k for k in range(len(so_far))},
        compiler_params=pltpu.CompilerParams(vmem_limit_bytes=VMEM_LIMIT),
    )(at.reshape(1), block, block, block, block, *so_far)


def gather_ctx(a, count, c):
    if count != 4:
        return lax.all_gather(a, "ctx", axis=0, tiled=True)
    rows = a.shape[0]
    ring = [(0, 1), (1, 3), (3, 2), (2, 0)]
    origins = [c, table((2, 0, 3, 1), c), 3 - c, table((1, 3, 0, 2), c)]
    out = jnp.zeros((rows * count, a.shape[1]), a.dtype)
    for step in range(4):
        out = lax.dynamic_update_slice_in_dim(out, a, origins[step] * rows, axis=0)
        if step < 3:
            a = lax.ppermute(a, "ctx", ring)
    return out


def gather_small(a, count, c):
    out = jnp.zeros((count, a.shape[0]), a.dtype)
    out = lax.dynamic_update_slice_in_dim(out, a[None], c, axis=0)
    return sum_ctx(out, count).reshape(-1)


def scatter_ctx(a, count, c):
    rows = a.shape[0] // count
    if count != 4:
        return lax.psum_scatter(a, "ctx", scatter_dimension=0, tiled=True)
    total = lax.dynamic_slice_in_dim(a, c * rows, rows, axis=0)
    sent = [
        lax.dynamic_slice_in_dim(a, (c ^ d) * rows, rows, axis=0).astype(BF16)
        for d in (3, 2, 1)
    ]
    for d, block in zip((3, 2, 1), sent):
        total = total + swap_ctx(block, count, d).astype(F32)
    return total


def line_sum(a):
    return lax.psum(a, "ctx").astype(F32)


def share_sums(a, count, c, *meanwhile):
    rows = a.shape[0] // count

    def share(index):
        return lax.dynamic_slice_in_dim(a, index * rows, rows, axis=0)

    total = after(share(c).astype(F32), *meanwhile)
    for d in (3, 2, 1):
        total = total + swap_ctx(share(c ^ d), count, d).astype(F32)
    return total.astype(BF16)


def shares_back(total, count, c, *meanwhile):
    rows = total.shape[0]
    out = after(jnp.zeros((rows * count, total.shape[1]), total.dtype), *meanwhile)
    for d in (3, 2, 1, 0):
        block = swap_ctx(total, count, d) if d else total
        out = lax.dynamic_update_slice_in_dim(out, block, (c ^ d) * rows, axis=0)
    return out


def sum_all(a, count, *behind):
    a = a + swap_core(a)
    a = a + swap_y(a)
    a = sum_ctx(a, count)
    return a + swap_x(after(a, *behind))


def sum_ctx(a, count):
    step = 1
    while step < count:
        a = a + lax.ppermute(a, "ctx", [(i, i ^ step) for i in range(count)])
        step *= 2
    return a


def per_device(
    hidden_in, teacher, w_query, w_key, w_value, w_out, w_gate, w_up, w_down,
    attn_gain, ffn_gain, segment_ids, parents, positions, valid_mask,
):
    rows, width = hidden_in.shape
    half = width // 2
    quarter = rows // 4
    count = lax.axis_size("ctx")
    f, c, t = (lax.axis_index(a) for a in ("fsdp", "ctx", "tp"))
    tree_len = rows * count
    unit = tree_len // 20
    trunk = 8 * unit
    nk = w_key.shape[1] // HD
    eighth = w_gate.shape[1] // 2
    part = eighth // 2
    parity = c % 2
    first = f == 0

    def turned(a):
        return jnp.where(first, a, halves_swapped(a))

    def reordered(a):
        cols = a.shape[1]
        a = a.reshape(2, 2, quarter, cols)
        a = jnp.where(t < 2, a, jnp.concatenate([a[1:], a[:1]], axis=0))
        a = jnp.where(t % 2 == 0, a, jnp.concatenate([a[:, 1:], a[:, :1]], axis=1))
        return a.reshape(rows, cols)

    def own_rows(a):
        return lax.dynamic_slice_in_dim(a, t * quarter, quarter, axis=0)

    def gather_tp(x):
        over_core, over_y = swap_core(x), swap_y(x)
        return [x, over_core, over_y, swap_core(over_y)]

    def gather_plane(x):
        flipped = halves_swapped(x)
        over_x = swap_x(flipped)
        group = [x, swap_y(x), over_x, swap_y(over_x) if CFG.get('e_relay') else swap_xy(flipped)]
        return group + [swap_core(a) for a in group]

    def gather_all(x):
        return lax.all_gather(turned(x), ("fsdp", "ctx", "tp"), axis=0, tiled=True)

    def halves_tp(product, a):
        cols = a.shape[1]
        blocks = a.reshape(2, 2, quarter, cols)
        sent = swap_core(product(blocks[:, 1].reshape(2 * quarter, cols)).astype(BF16))
        kept = product(blocks[:, 0].reshape(2 * quarter, cols)) + sent.astype(F32)
        return kept[:quarter], kept[quarter:].astype(BF16)

    def scatter_out(lefts, nears, fars, contract):
        sent = swap_core(out_call(lefts, nears, fars, contract, 1))
        return out_call(lefts, nears, fars, contract, 0, sent)

    def scatter_sum(products, *meanwhile):
        kept, to_y, to_x, to_xy = products
        over_xy, over_y, over_x = swap_xy(to_xy), swap_y(to_y), swap_x(to_x)
        kept = after(kept, *meanwhile)
        return kept + over_y.astype(F32) + over_x.astype(F32) + over_xy.astype(F32)

    far_key, far_value = swap_x(w_key), swap_x(w_value)
    far_gains = swap_x(jnp.stack([attn_gain, ffn_gain]))
    gain_attn = jnp.concatenate([attn_gain, far_gains[0]]).astype(F32)
    gain_ffn = jnp.concatenate([ffn_gain, far_gains[1]]).astype(F32)
    far_query = swap_x(after(w_query, far_key, far_value))
    far_out = swap_x(after(w_out, far_query))

    sends = []

    def exchanged(w, axis, share, *behind):
        def cut(index, which):
            return lax.dynamic_slice_in_dim(w, index * eighth + which * part, part, axis=axis)

        sends.append(cut(1 - f, parity))
        got = swap_x(after(sends[-1], *behind))
        if not share:
            sends.append(cut(1 - f, 1 - parity))
            other = swap_x(after(sends[-1], *behind))
        else:
            other = swap_ctx(got, count, 1)
        return (cut(f, parity), got), (cut(f, 1 - parity), other)

    gate_p, gate_o = exchanged(w_gate, 1, True, far_out)
    up_p, up_o = exchanged(w_up, 1, True, far_out if CFG.get('e_two') else gate_p[1])

    labels = jnp.arange(parents.shape[0], dtype=jnp.int32)
    seg = segment_ids[::BLK]
    parent = jnp.sum(jnp.where(seg[:, None] == labels[None, :], parents[None, :], 0), axis=1)
    grand = jnp.sum(jnp.where(parent[:, None] == labels[None, :], parents[None, :], 0), axis=1)
    all_seg = gather_small(seg, count, c)
    spots = jnp.arange(all_seg.shape[0], dtype=jnp.int32)
    parent_spot = jnp.min(
        jnp.where(all_seg[None, :] == parent[:, None], spots[None, :], all_seg.shape[0] - 1),
        axis=1,
    )
    slot = c * rows + jnp.arange(seg.shape[0], dtype=jnp.int32) * BLK
    branch_or_leaf = parent >= 0
    leaf = branch_or_leaf & (grand >= 0)
    own_ok = branch_or_leaf & (valid_mask[::BLK] == 1)
    nothing = jnp.zeros_like(slot)
    meta = jnp.stack(
        [
            slot,
            jnp.where(branch_or_leaf, slot // unit * unit, 0),
            own_ok.astype(jnp.int32),
            jnp.where(leaf, parent_spot * BLK, 0),
            leaf.astype(jnp.int32),
            nothing,
            nothing,
            nothing,
        ],
        axis=1,
    ).reshape(-1)

    valid_f = valid_mask.astype(F32)
    valid_count = jnp.sum(valid_f).reshape(1, 1)
    valid_count = sum_ctx(valid_count + swap_x(valid_count), count)[0, 0]
    cosine, sine = rope_tables(positions)

    hidden = turned(hidden_in)
    normed = rms_scale(hidden.astype(F32), gain_attn).astype(BF16)
    near_normed, far_normed = normed[:, :half], normed[:, half:]
    normed_in, meta, valid_count = lax.optimization_barrier((normed, meta, valid_count))
    normed_in = after(normed_in, *on('early', *sends))
    kv = proj_call(
        normed_in, cosine, sine, (True, False), (w_key, far_key, w_value, far_value)
    )
    query = proj_call(after(normed_in, kv), cosine, sine, (True,), (w_query, far_query))
    kv_all = gather_ctx(kv, count, c)
    query_in, out_full = lax.optimization_barrier(
        (query, jnp.concatenate([w_out, far_out], axis=1))
    )
    attended, context, total = fwd_call(meta, query_in, kv_all, nk, unit, trunk)
    attended = after(reordered(attended), *on('e_gp', gate_p[1]))
    kept, to_y = halves_tp(lambda a: dot(a, out_full), attended)
    attn_out = kept + swap_y(to_y).astype(F32)

    hidden_own = own_rows(hidden).astype(F32)
    middle = hidden_own + attn_out
    normed_own = after(rms_scale(middle, gain_ffn).astype(BF16), *on('e_up', up_p[1]), *on('e_go', gate_o[1]))
    normed_pieces = gather_plane(normed_own)
    down_p, down_o = exchanged(w_down, 0, bool(CFG.get('e_share')), *on('e_after', normed_pieces[2]), *on('e_after2', normed_pieces[3]), up_p[1])
    *act_p, normed_ffn = up_call(normed_pieces, *gate_p, *up_p)
    shares = count == 4
    normed_ffn = after(normed_ffn, *on('e_hook', down_p[1]), *on('e_hook2', up_o[1]))
    act_o = list(up_call([normed_ffn], *gate_o, *up_o))
    output_f = middle + scatter_sum(
        scatter_out([act_p[2], act_o[2]], [down_p[0], down_o[0]], [down_p[1], down_o[1]], 0)
    )

    deviation = output_f - turned(own_rows(teacher)).astype(F32)
    valid_own = lax.dynamic_slice_in_dim(valid_f, t * quarter, quarter, axis=0)
    error_sum = jnp.sum(valid_own * jnp.mean(deviation * deviation, axis=1))
    tokens_all = rows * lax.axis_size("fsdp") * count
    loss_factor = float(width * tokens_all // 2)
    grad_output = loss_factor * 2.0 / width * valid_own[:, None] * deviation / valid_count

    grad_own = grad_output.astype(BF16)
    grad_pieces = gather_plane(grad_own)
    if shares:
        normed_all, grad_all = gather_all(after(normed_own, *on('e_ag', normed_pieces[3]), *on('e_ag2', down_p[1]))), gather_all(grad_own)
        place = f.reshape(1)
    gg_p, gu_p, grad_ffn = act_back_call(grad_pieces, *down_p, act_p[0], act_p[1])
    gg_o, gu_o = act_back_call([grad_ffn], *down_o, act_o[0], act_o[1])
    products = scatter_out(
        [gg_p, gu_p, gg_o, gu_o],
        [gate_p[0], up_p[0], gate_o[0], up_o[0]],
        [gate_p[1], up_p[1], gate_o[1], up_o[1]],
        1,
    )
    meanwhile = ()
    if shares:
        ahead_p = all_up_call(after(place, products[0]), normed_all, rows, (*gate_p, *up_p))
        meanwhile = ahead_p
    grad_normed_ffn = scatter_sum(products, *meanwhile)

    def joined(blocks, axis):
        shape = list(blocks[0][0].shape)
        shape[axis] *= 4
        out = jnp.zeros(shape, F32)
        for block, index, which in blocks:
            out = lax.dynamic_update_slice_in_dim(
                out, block.astype(F32), index * eighth + which * part, axis=axis
            )
        return out

    _, norm_ffn_back = jax.vjp(rms_scale, middle, gain_ffn)
    grad_middle_part, grad_ffn_gain = norm_ffn_back(grad_normed_ffn)
    grad_middle = grad_output + grad_middle_part

    grad_attn = gather_tp(grad_middle.astype(BF16))
    if shares:
        if not CFG.get('ahead_late'):
            ahead_o = all_up_call(after(place, grad_middle), normed_all, rows, (*gate_o, *up_o))
            grad_attn[0] = after(grad_attn[0], *ahead_o)
    grad_attn = jnp.concatenate(grad_attn, axis=0)
    out_sent = swap_x(dot_tn(attended, grad_attn[:, half:], BF16))
    out_kept = dot_tn(attended, grad_attn[:, :half])
    grad_context = reordered(dot_nt(grad_attn, out_full))
    if shares and CFG.get('c_all'):
        grad_context, grad_all = lax.optimization_barrier((grad_context, grad_all))
    grad_query, key_terms, value_terms = bwd_call(
        meta, query, kv_all, grad_context, context, total, cosine, sine, nk, unit, trunk
    )
    query_far = dot_tn(far_normed, grad_query, BF16)
    query_sent, query_kept = swap_x(query_far), dot_tn(near_normed, grad_query)
    out_kept = after(out_kept, grad_query)
    out_part = (out_kept + out_sent.astype(F32)).astype(BF16)
    if shares:
        place = after(place, grad_query, *on('a_qfar', query_far), *on('a_qkept', query_kept), *on('a_out', out_part), *on('a_qsent', query_sent))
        if CFG.get('ahead_late'):
            ahead_o = all_up_call(place, normed_all, rows, (*gate_o, *up_o))
            place = after(place, *ahead_o)
        done, *back_p = far_grads_call(place, normed_all, grad_all, rows, down_p, ahead_p)
    else:

        def ordered(a, b):
            return jnp.where(parity == 0, a, b), jnp.where(parity == 0, b, a)

        def summed(pair_p, pair_o, axis):
            blocks = []
            for which, (near, far) in enumerate(zip(*(ordered(a, b) for a, b in zip(pair_p, pair_o)))):
                blocks.append((line_sum(near), f, which))
                blocks.append((line_sum(swap_x(far)), 1 - f, which))
            return joined(blocks, axis)

        def columns(g):
            return dot_tn(normed_ffn[:, :half], g, BF16), dot_tn(normed_ffn[:, half:], g, BF16)

        def lines(a):
            return dot_tn(a, grad_ffn[:, :half], BF16), dot_tn(a, grad_ffn[:, half:], BF16)

        grad_gate_w = summed(columns(gg_p), columns(gg_o), 1)
        grad_up_w = summed(columns(gu_p), columns(gu_o), 1)
        grad_down_w = summed(lines(act_p[2]), lines(act_o[2]), 0)

    kv_sums = scatter_ctx(jnp.concatenate([key_terms, value_terms], axis=1), count, c)
    if shares:
        kv_sums = after(kv_sums, done, *on('kv_q', query_sent))
    grad_kv = dkv_call(kv_sums, cosine, sine, nk)
    kv_far = dot_tn(far_normed, grad_kv, BF16)
    kv_sent, kv_kept = swap_x(kv_far), dot_tn(near_normed, grad_kv)
    query_part = (query_kept + query_sent.astype(F32)).astype(BF16)
    kv_part = None if CFG.get('kv_late') and shares else (kv_kept + kv_sent.astype(F32)).astype(BF16)
    grad_query_w, grad_out_w = lax.psum((query_part, out_part), "ctx")
    nears = jnp.concatenate([w_query, w_key, w_value], axis=1)
    fars = jnp.concatenate([far_query, far_key, far_value], axis=1)
    kept, to_y = halves_tp(
        lambda a: jnp.concatenate([dot_nt(a, nears), dot_nt(a, fars)], axis=1),
        reordered(jnp.concatenate([grad_query, grad_kv], axis=1)),
    )
    if shares:
        over_p = swap_x(after(done, *on('x_kv', kv_far), *on('x_q', query_sent)))
        place = after(place, done, *on('b_y', to_y), *on('b_q', query_part), *on('b_kv', kv_part), *on('b_kvkept', kv_kept), *on('b_out', out_part))
        far, *back_o = far_grads_call(place, normed_all, grad_all, rows, down_o, ahead_o)
        over_o = swap_x(far)
        over_y = swap_y(to_y)
        place = after(place, far)
        if CFG.get('kv_late'):
            kv_part = (after(kv_kept, far) + kv_sent.astype(F32)).astype(BF16)
            place = after(place, *on('n_kv', kv_part))
        else:
            kv_shares = share_sums(kv_part, count, c, far)
            place = after(place, *on('n_kv', kv_shares))
        place = after(place, *on('n_y', over_y), *on('n_p', over_p))
        near_p, near_o = near_grads_call(
            place, normed_all, grad_all, 2 * rows, (ahead_p[2], *back_p, ahead_o[2], *back_o)
        )
        meanwhile = (near_p,)
        weights = place_call(2 * (1 - f) + parity, over_p)
        weights = place_call(2 * f + parity, near_p, weights)
        weights = place_call(2 * f + 1 - parity, near_o, weights)
        grad_gate_w, grad_up_w, grad_down_w = place_call(
            2 * (1 - f) + 1 - parity, over_o, weights
        )
    else:
        meanwhile = ()
        over_y = swap_y(to_y)
    if shares:
        if CFG.get('kv_late'):
            kv_shares = share_sums(kv_part, count, c, *meanwhile, *on('s_ar', grad_query_w, grad_out_w))
            grad_kv_w = gather_ctx(kv_shares, count, c).astype(F32)
        else:
            grad_kv_w = shares_back(kv_shares, count, c, *meanwhile, *on('s_ar', grad_query_w, grad_out_w)).astype(F32)
    else:
        grad_kv_w = line_sum(kv_part)
    grad_normed = kept + over_y.astype(F32)
    _, norm_attn_back = jax.vjp(rms_scale, hidden_own, gain_attn)
    grad_hidden_part, grad_attn_gain = norm_attn_back(grad_normed)
    grad_hidden = after(grad_middle, *on('h_near', *meanwhile)) + grad_hidden_part

    def whole_rows(x, kind, *behind):
        pair = after(jnp.concatenate([x, swap_y(x)], axis=0), *behind)
        out = jnp.zeros((rows, width), kind)
        for k, blocks in enumerate((pair, swap_core(pair))):
            for y in range(2):
                block = blocks[y * quarter : (y + 1) * quarter].astype(kind)
                out = lax.dynamic_update_slice_in_dim(
                    out, block, (t ^ (2 * y + k)) * quarter, axis=0
                )
        return out

    small = jnp.concatenate(
        [turned(grad_attn_gain), turned(grad_ffn_gain), jnp.full((HD,), error_sum, F32)]
    ).reshape(1, -1)
    small = after(small, *on('s_near', *meanwhile))
    small = sum_all(small, count, *(on('s_last', over_o) if shares else ()))[0]
    loss_value = small[2 * width] / valid_count
    own_attn_gain = lax.dynamic_slice_in_dim(small[:width], f * half, half)
    own_ffn_gain = lax.dynamic_slice_in_dim(small[width : 2 * width], f * half, half)
    return (
        whole_rows(after(turned(output_f).astype(BF16), *on('o_q', grad_query), *on('o_ffn', grad_ffn), *(on('o_done', done) if shares else ()), *on('o_near', *meanwhile)), BF16, *on('ow_near', *meanwhile)),
        loss_value,
        whole_rows(turned(grad_hidden).astype(BF16), F32, *on('w_near', *meanwhile)),
        grad_query_w.astype(F32),
        grad_kv_w[:, : nk * HD],
        grad_kv_w[:, nk * HD :],
        grad_out_w.astype(F32),
        grad_gate_w,
        grad_up_w,
        grad_down_w,
        own_attn_gain,
        own_ffn_gain,
    )


def solution(mesh):
    tokens = P(("fsdp", "ctx"))
    token_rows = P(("fsdp", "ctx"), None)
    column = P("fsdp", "tp")
    row = P("tp", "fsdp")
    gain = P("fsdp")
    weights = (column, column, column, row, column, column, row, gain, gain)
    return jax.shard_map(
        per_device,
        mesh=mesh,
        in_specs=(token_rows, token_rows, *weights, tokens, P(), tokens, tokens),
        out_specs=(token_rows, P(), token_rows, *weights),
        check_vma=False,
    )
```
